128 devices in a mesh: dp: 16 (over y_hi, x, core), seq: 8 (over y_lo, z).
Axes of the slice: x: 4, y: 4 (y_hi: 2, y_lo: 2; y = y_hi * 2 + y_lo), z: 4, core: 2. Of those that a mesh axis runs over, the one named last changes fastest.
Arguments:
- tokens: bfloat16 [16384, 2048], P(('dp', 'seq')), may hold values from -6 to 6
- cotangent: bfloat16 [16384, 2048], P(('dp', 'seq')), may hold values from -6 to 6
- doc_lengths: int32 [16, 3], P('dp'), may hold values from 1 to 1022, as said below
- entry_weight: float32 [2048, 1536], P('dp')
- entry_first: float32 [2048, 1536], P('dp')
- entry_second: float32 [2048, 1536], P('dp'), as said below
- entry_average: float32 [2048, 1536], P('dp')
- query_weight: float32 [1024, 4096], P('dp', 'seq')
- query_first: float32 [1024, 4096], P('dp', 'seq')
- query_second: float32 [1024, 4096], P('dp', 'seq'), as said below
- query_average: float32 [1024, 4096], P('dp', 'seq')
- out_weight: float32 [2048, 4096], P('dp', 'seq')
- out_first: float32 [2048, 4096], P('dp', 'seq')
- out_second: float32 [2048, 4096], P('dp', 'seq'), as said below
- out_average: float32 [2048, 4096], P('dp', 'seq')
- ffn_weight: float32 [2048, 3, 5632], P('dp', None, 'seq')
- ffn_first: float32 [2048, 3, 5632], P('dp', None, 'seq')
- ffn_second: float32 [2048, 3, 5632], P('dp', None, 'seq'), as said below
- ffn_average: float32 [2048, 3, 5632], P('dp', None, 'seq')
- norm_gains: float32 [5120], replicated, may hold values from -0.625 to 0.625
- gains_first: float32 [5120], replicated, may hold values from -80 to 80
- gains_second: float32 [5120], replicated, may hold values from 868.352 to 3440.64
- gains_average: float32 [5120], replicated, may hold values from -0.625 to 0.625
Outputs:
- mixed: bfloat16 [16384, 2048], P(('dp', 'seq'))
- input_grad: float32 [16384, 2048], P(('dp', 'seq'))
- entry_grad: float32 [2048, 1536], P('dp')
- entry_moment: float32 [2048, 1536], P('dp')
- entry_squares: float32 [2048, 1536], P('dp')
- entry_master: float32 [2048, 1536], P('dp')
- entry_smooth: float32 [2048, 1536], P('dp')
- query_grad: float32 [1024, 4096], P('dp', 'seq')
- query_moment: float32 [1024, 4096], P('dp', 'seq')
- query_squares: float32 [1024, 4096], P('dp', 'seq')
- query_master: float32 [1024, 4096], P('dp', 'seq')
- query_smooth: float32 [1024, 4096], P('dp', 'seq')
- out_grad: float32 [2048, 4096], P('dp', 'seq')
- out_moment: float32 [2048, 4096], P('dp', 'seq')
- out_squares: float32 [2048, 4096], P('dp', 'seq')
- out_master: float32 [2048, 4096], P('dp', 'seq')
- out_smooth: float32 [2048, 4096], P('dp', 'seq')
- ffn_grad: float32 [2048, 3, 5632], P('dp', None, 'seq')
- ffn_moment: float32 [2048, 3, 5632], P('dp', None, 'seq')
- ffn_squares: float32 [2048, 3, 5632], P('dp', None, 'seq')
- ffn_master: float32 [2048, 3, 5632], P('dp', None, 'seq')
- ffn_smooth: float32 [2048, 3, 5632], P('dp', None, 'seq')
- gains_grad: float32 [5120], replicated
- gains_moment: float32 [5120], replicated
- gains_squares: float32 [5120], replicated
- gains_master: float32 [5120], replicated
- gains_smooth: float32 [5120], replicated
The draws below stay inside these ranges and needn't reach their ends.
Inputs may be any that keep to these rules, and one draw needn't show every extreme that they name: `doc_lengths`: each row sums to 1024; its first and last lengths are below 128. `entry_second`: entries are positive. `query_second`: entries are positive. `out_second`: entries are positive. `ffn_second`: entries are positive.
All inputs are finite; a program needn't handle non-finite values.
Results may differ from the reference program's by a relative error of at most 0.023.
Values may be sent and summed in bfloat16 or wider, within the bound.
No kernel may reach another device: no remote copies, remote signals or barrier semaphores. Data moves between devices by JAX's collectives and lax.ppermute only.
A program may use at most 192 MiB of HBM per device.

```python
import math
import jax
import jax.numpy as jnp
from jax import lax

D = 2048
QLAT = 1024
HEADS = 16
HDIM = 256
FF = 5632
SEQ_LEN = 1024
STEP = 10
TOKENS = 16384
N_DP = 16
N_SEQ = 8


def root_tokens():
    return math.sqrt(TOKENS)


def bounded_normal(key, shape, scales):
    return jax.random.truncated_normal(key, -3.0, 3.0, shape, jnp.float32) * scales


def second_moments(key, shape, levels):
    spread = jnp.exp(jax.random.uniform(key, shape, jnp.float32, 0.0, math.log(4.0)))
    return 0.053 * levels * levels * spread


def ffn_scales():
    return jnp.array([D ** (-0.5), D ** (-0.5), FF ** (-0.5)], jnp.float32)[None, :, None]


def ffn_levels():
    return jnp.array([0.4, 0.4, 0.6], jnp.float32)[None, :, None] * root_tokens()


def draw_entry_weight(key, part):
    key = jax.random.fold_in(key, 1)
    return bounded_normal(key, (D, QLAT + 2 * HDIM), D ** (-0.5))


def draw_entry_average(key, part):
    key = jax.random.fold_in(key, 2)
    return bounded_normal(key, (D, QLAT + 2 * HDIM), D ** (-0.5))


def draw_entry_first(key, part):
    key = jax.random.fold_in(key, 3)
    return bounded_normal(key, (D, QLAT + 2 * HDIM), 0.11 * 1.5 * root_tokens())


def draw_entry_second(key, part):
    key = jax.random.fold_in(key, 4)
    return second_moments(key, (D, QLAT + 2 * HDIM), 1.5 * root_tokens())


def draw_query_weight(key, part):
    key = jax.random.fold_in(key, 5)
    return bounded_normal(key, (QLAT, HEADS * HDIM), QLAT ** (-0.5))


def draw_query_average(key, part):
    key = jax.random.fold_in(key, 6)
    return bounded_normal(key, (QLAT, HEADS * HDIM), QLAT ** (-0.5))


def draw_query_first(key, part):
    key = jax.random.fold_in(key, 7)
    return bounded_normal(key, (QLAT, HEADS * HDIM), 0.11 * 0.4 * root_tokens())


def draw_query_second(key, part):
    key = jax.random.fold_in(key, 8)
    return second_moments(key, (QLAT, HEADS * HDIM), 0.4 * root_tokens())


def draw_out_weight(key, part):
    key = jax.random.fold_in(key, 10)
    return bounded_normal(key, (D, HEADS * HDIM), 4.0 * (HEADS * HDIM) ** (-0.5))


def draw_out_average(key, part):
    key = jax.random.fold_in(key, 11)
    return bounded_normal(key, (D, HEADS * HDIM), 4.0 * (HEADS * HDIM) ** (-0.5))


def draw_out_first(key, part):
    key = jax.random.fold_in(key, 12)
    return bounded_normal(key, (D, HEADS * HDIM), 0.11 * 0.3 * root_tokens())


def draw_out_second(key, part):
    key = jax.random.fold_in(key, 13)
    return second_moments(key, (D, HEADS * HDIM), 0.3 * root_tokens())


def draw_ffn_weight(key, part):
    key = jax.random.fold_in(key, 14)
    return bounded_normal(key, (D, 3, FF), ffn_scales())


def draw_ffn_average(key, part):
    key = jax.random.fold_in(key, 15)
    return bounded_normal(key, (D, 3, FF), ffn_scales())


def draw_ffn_first(key, part):
    key = jax.random.fold_in(key, 16)
    return bounded_normal(key, (D, 3, FF), 0.11 * ffn_levels())


def draw_ffn_second(key, part):
    key = jax.random.fold_in(key, 17)
    return second_moments(key, (D, 3, FF), ffn_levels())


def draw_doc_lengths(key, part):
    key = jax.random.fold_in(key, 9)
    key_first, key_last, key_pick = jax.random.split(key, 3)
    edge = SEQ_LEN // N_SEQ
    head_len = jax.random.randint(key_first, (N_DP,), 1, edge)
    tail_len = jax.random.randint(key_last, (N_DP,), 1, edge)
    picked = jax.random.randint(key_pick, (), 0, N_DP)
    group_ids = jnp.arange(N_DP, dtype=jnp.int32)
    head_len = jnp.where(group_ids == picked, 1, head_len)
    tail_len = jnp.where(group_ids == picked, 1, tail_len)
    middle_len = SEQ_LEN - head_len - tail_len
    return jnp.stack([head_len, middle_len, tail_len], axis=1).astype(jnp.int32)


def level_of(rng, extent, cuts, least, high):
    factor_of = 1.0
    for axis_at, shards_of in cuts:
        heights = jax.random.uniform(jax.random.fold_in(jax.random.fold_in(rng, 6), axis_at), (shards_of,), jnp.float32, least / len(cuts), high / len(cuts))
        factor_of = factor_of * jnp.repeat(jnp.exp(heights), extent[axis_at] // shards_of).reshape((-1,) + (1,) * (len(extent) - 1 - axis_at))
    return factor_of


def bell_draw(key, shape, scale, bound, cuts=(), held_as=jnp.bfloat16):
    values = scale * jax.random.normal(key, shape, jnp.float32)
    if cuts:
        values = values * level_of(key, shape, cuts, -0.22, 0.18)
    return jnp.clip(values, -bound, bound).astype(held_as)


def setup_inputs(seed: int = 0) -> dict:
    key_of = jax.random.split(jax.random.key(seed), 24)
    return {
        "tokens": bell_draw(key_of[0], (TOKENS, D), 1.0, 6.0, ((0, 128),)),
        "cotangent": bell_draw(key_of[1], (TOKENS, D), 1.0, 6.0, ((0, 128),)),
        "doc_lengths": draw_doc_lengths(jax.random.fold_in(key_of[23], 71), 0),
        "entry_weight": draw_entry_weight(jax.random.fold_in(key_of[23], 71), 0),
        "entry_first": draw_entry_first(jax.random.fold_in(key_of[23], 71), 0),
        "entry_second": draw_entry_second(jax.random.fold_in(key_of[23], 71), 0),
        "entry_average": draw_entry_average(jax.random.fold_in(key_of[23], 71), 0),
        "query_weight": draw_query_weight(jax.random.fold_in(key_of[23], 71), 0),
        "query_first": draw_query_first(jax.random.fold_in(key_of[23], 71), 0),
        "query_second": draw_query_second(jax.random.fold_in(key_of[23], 71), 0),
        "query_average": draw_query_average(jax.random.fold_in(key_of[23], 71), 0),
        "out_weight": draw_out_weight(jax.random.fold_in(key_of[23], 71), 0),
        "out_first": draw_out_first(jax.random.fold_in(key_of[23], 71), 0),
        "out_second": draw_out_second(jax.random.fold_in(key_of[23], 71), 0),
        "out_average": draw_out_average(jax.random.fold_in(key_of[23], 71), 0),
        "ffn_weight": draw_ffn_weight(jax.random.fold_in(key_of[23], 71), 0),
        "ffn_first": draw_ffn_first(jax.random.fold_in(key_of[23], 71), 0),
        "ffn_second": draw_ffn_second(jax.random.fold_in(key_of[23], 71), 0),
        "ffn_average": draw_ffn_average(jax.random.fold_in(key_of[23], 71), 0),
        "norm_gains": bell_draw(key_of[19], (2 * D + QLAT,), 0.1, 0.625, (), jnp.float32),
        "gains_first": bell_draw(key_of[20], (2 * D + QLAT,), (0.11 * TOKENS ** 0.5), 80.0, (), jnp.float32),
        "gains_second": jnp.clip(jnp.exp(jax.random.uniform(key_of[21], (2 * D + QLAT,), jnp.float32, math.log(868.352), math.log(3440.64))), 868.352, 3440.64),
        "gains_average": bell_draw(key_of[22], (2 * D + QLAT,), 0.1, 0.625, (), jnp.float32),
    }


EPS = 1e-05
THETA = 10000.0
BETA_ONE = 0.9
BETA_TWO = 0.95
ADAM_EPS = 1e-08
ENTRY_RATE = 0.03
QUERY_RATE = 0.04
OUT_RATE = 0.08
FFN_RATE = 0.03
GAIN_RATE = 0.1
DECAY = 0.1
MASKED = -1e+30

@jax.custom_vjp
def low(v):
    return lax.optimization_barrier(v.astype(jnp.bfloat16)).astype(jnp.float32)

@jax.custom_vjp
def low_back(v):
    return v

def low_keep(v):
    return (low(v), None)

def low_pass(kept, grad):
    return (grad,)

def back_keep(v):
    return (v, None)

def back_low(kept, grad):
    return (low(grad),)
low.defvjp(low_keep, low_pass)
low_back.defvjp(back_keep, back_low)

def exact_dot(left, right):
    return jnp.dot(left, right, precision=lax.Precision.HIGHEST)

def doc_layout(lengths, token_count):
    ends = jnp.cumsum(lengths).astype(jnp.int32)
    starts = (ends - lengths).astype(jnp.int32)
    places = jnp.arange(token_count, dtype=jnp.int32)
    inside = (places[:, None] >= starts[None, :]) & (places[:, None] < ends[None, :])
    labels = jnp.arange(lengths.shape[0], dtype=jnp.int32)
    segment = lax.optimization_barrier(jnp.sum(jnp.where(inside, labels[None, :], 0), axis=1)).astype(jnp.int32)
    offset = places - lax.optimization_barrier(jnp.sum(jnp.where(inside, starts[None, :], 0), axis=1)).astype(jnp.int32)
    return (places, segment, offset)

def rope_tables(offset, half_dim):
    freqs = THETA ** (-jnp.arange(half_dim, dtype=jnp.float32) * 2.0 / (2.0 * half_dim))
    angles = offset.astype(jnp.float32)[:, None] * freqs[None, :]
    return (jnp.cos(angles), jnp.sin(angles))

def rotate(values, cos_table, sine_table):
    half_dim = values.shape[-1] // 2
    left_half = values[..., :half_dim]
    right_half = values[..., half_dim:]
    return jnp.concatenate([left_half * cos_table - right_half * sine_table, left_half * sine_table + right_half * cos_table], axis=-1)

def rms_scale(values):
    return lax.rsqrt(lax.optimization_barrier(jnp.mean(values * values, axis=-1, keepdims=True)) + EPS)

def adamw_step(weight, moment, squares, grad, rate, decay):
    moment_new = BETA_ONE * moment + (1.0 - BETA_ONE) * grad
    squares_new = BETA_TWO * squares + (1.0 - BETA_TWO) * grad * grad
    first_fix = 1.0 - BETA_ONE ** STEP
    second_fix = 1.0 - BETA_TWO ** STEP
    update = moment_new / first_fix / (jnp.sqrt(squares_new / second_fix) + ADAM_EPS)
    master = weight - rate * (update + decay * weight)
    return (moment_new, squares_new, master)

def layer_forward(inputs, entry_w, query_w, out_w, ffn_w, gains_w, places, segment, cos_table, sine_table):
    token_count = inputs.shape[0]
    gain_one = 1.0 + gains_w[:D]
    gain_query = 1.0 + gains_w[D:D + QLAT]
    gain_two = 1.0 + gains_w[D + QLAT:]
    entry_low = low(entry_w)
    query_low = low(query_w)
    out_low = low(out_w)
    ffn_low = low(ffn_w)
    normed_one = low(inputs * rms_scale(inputs) * gain_one)
    first_proj = low_back(exact_dot(normed_one, entry_low))
    latent = first_proj[:, :QLAT]
    normed_query = low(latent * rms_scale(latent) * gain_query)
    query_pre = low_back(exact_dot(normed_query, query_low))
    queries = low(rotate(query_pre.reshape(token_count, HEADS, HDIM), cos_table[:, None, :], sine_table[:, None, :]))
    keys_rot = low(rotate(first_proj[:, QLAT:QLAT + HDIM], cos_table, sine_table))
    values_low = low(first_proj[:, QLAT + HDIM:])
    block_rows = min(512, token_count)
    blocks_count = token_count // block_rows

    def attend(pieces):
        query_rows, seg_rows, place_rows = pieces
        scores = jnp.einsum('qhd,kd->qhk', query_rows, keys_rot, precision=lax.Precision.HIGHEST) * HDIM ** (-0.5)
        scores = low_back(scores)
        allowed = (seg_rows[:, None] == segment[None, :]) & (place_rows[:, None] >= places[None, :])
        scores = jnp.where(allowed[:, None, :], scores, MASKED)
        shifted = jnp.exp(scores - lax.optimization_barrier(jnp.max(scores, axis=-1, keepdims=True)))
        weights = low(shifted / lax.optimization_barrier(jnp.sum(shifted, axis=-1, keepdims=True)))
        return jnp.einsum('qhk,kd->qhd', weights, values_low, precision=lax.Precision.HIGHEST)
    attended = lax.map(jax.checkpoint(attend), (queries.reshape(blocks_count, block_rows, HEADS, HDIM), segment.reshape(blocks_count, block_rows), places.reshape(blocks_count, block_rows)))
    attended = low(low_back(attended.reshape(token_count, HEADS * HDIM)))
    branch = low_back(exact_dot(attended, out_low.T))
    middle = inputs + branch
    normed_two = low(middle * rms_scale(middle) * gain_two)
    gate_up = low_back(exact_dot(normed_two, ffn_low[:, :2, :].reshape(D, 2 * FF)))
    hidden = low(jax.nn.silu(gate_up[:, :FF]) * gate_up[:, FF:])
    return middle + low_back(exact_dot(hidden, ffn_low[:, 2, :].T))

def reference(tokens, cotangent, doc_lengths, entry_weight, entry_first, entry_second, entry_average, query_weight, query_first, query_second, query_average, out_weight, out_first, out_second, out_average, ffn_weight, ffn_first, ffn_second, ffn_average, norm_gains, gains_first, gains_second, gains_average):
    groups_in = tokens.astype(jnp.float32).reshape(N_DP, SEQ_LEN, D)
    groups_back = cotangent.astype(jnp.float32).reshape(N_DP, SEQ_LEN, D)

    def group_step(totals, pieces):
        group_in, group_back, lengths = pieces
        places, segment, offset = doc_layout(lengths, SEQ_LEN)
        cos_table, sine_table = rope_tables(offset, HDIM // 2)

        def forward(inputs, entry_w, query_w, out_w, ffn_w, gains_w):
            return layer_forward(inputs, entry_w, query_w, out_w, ffn_w, gains_w, places, segment, cos_table, sine_table)
        result, pullback = jax.vjp(forward, group_in, entry_weight, query_weight, out_weight, ffn_weight, norm_gains)
        grads = pullback(group_back)
        totals = tuple((total + grad for total, grad in zip(totals, grads[1:])))
        return (totals, (result.astype(jnp.bfloat16), grads[0]))
    start_totals = (jnp.zeros_like(entry_weight), jnp.zeros_like(query_weight), jnp.zeros_like(out_weight), jnp.zeros_like(ffn_weight), jnp.zeros_like(norm_gains))
    totals, outputs = lax.scan(group_step, start_totals, (groups_in, groups_back, doc_lengths))
    entry_grad, query_grad, out_grad, ffn_grad, gains_grad = totals
    mixed_out = outputs[0].reshape(TOKENS, D)
    input_grad = outputs[1].reshape(TOKENS, D)
    average_keep = min(0.999, (1.0 + STEP) / (10.0 + STEP))
    entry_moment, entry_squares, entry_master = adamw_step(entry_weight, entry_first, entry_second, entry_grad, ENTRY_RATE, DECAY)
    query_moment, query_squares, query_master = adamw_step(query_weight, query_first, query_second, query_grad, QUERY_RATE, DECAY)
    out_moment, out_squares, out_master = adamw_step(out_weight, out_first, out_second, out_grad, OUT_RATE, DECAY)
    ffn_moment, ffn_squares, ffn_master = adamw_step(ffn_weight, ffn_first, ffn_second, ffn_grad, FFN_RATE, DECAY)
    gains_moment, gains_squares, gains_master = adamw_step(norm_gains, gains_first, gains_second, gains_grad, GAIN_RATE, 0.0)
    entry_smooth = average_keep * entry_average + (1.0 - average_keep) * entry_master
    query_smooth = average_keep * query_average + (1.0 - average_keep) * query_master
    out_smooth = average_keep * out_average + (1.0 - average_keep) * out_master
    ffn_smooth = average_keep * ffn_average + (1.0 - average_keep) * ffn_master
    gains_smooth = average_keep * gains_average + (1.0 - average_keep) * gains_master
    return (mixed_out, input_grad, entry_grad, entry_moment, entry_squares, entry_master, entry_smooth, query_grad, query_moment, query_squares, query_master, query_smooth, out_grad, out_moment, out_squares, out_master, out_smooth, ffn_grad, ffn_moment, ffn_squares, ffn_master, ffn_smooth, gains_grad, gains_moment, gains_squares, gains_master, gains_smooth)
```

```python
import functools

import jax
import jax.numpy as jnp
import numpy as np
from jax import lax
from jax.experimental import pallas as pl
from jax.experimental.pallas import tpu as pltpu
from jax.sharding import Mesh, PartitionSpec as P

D = 2048
QLAT = 1024
HDIM = 256
STEP = 10
EPS = 1e-05
THETA = 10000.0
BETA_ONE = 0.9
BETA_TWO = 0.95
ADAM_EPS = 1e-08
ENTRY_RATE = 0.03
QUERY_RATE = 0.04
OUT_RATE = 0.08
FFN_RATE = 0.03
GAIN_RATE = 0.1
DECAY = 0.1
MASKED = -1e30
SIZES = {"yh": 2, "x": 4, "c": 2, "yl": 2, "z": 4}
AXES = ("yh", "x", "c", "yl", "z")
BF = jnp.bfloat16
F32 = jnp.float32


def move(value, axes, source):
    dims = [SIZES[a] for a in axes]
    pairs = []
    for place in np.ndindex(*dims):
        src = source(dict(zip(axes, place)))
        src_place = [src[a] % SIZES[a] for a in axes]
        pairs.append((int(np.ravel_multi_index(src_place, dims)), int(np.ravel_multi_index(place, dims))))
    return lax.ppermute(value, axes, pairs)


def from_z(value, k):
    return move(value, ("z",), lambda d: {"z": d["z"] + k})


def from_x(value, k):
    return move(value, ("x",), lambda d: {"x": d["x"] + k})


def from_y(value, e):
    return move(value, ("yh", "yl"), lambda d: {"yh": d["yh"] ^ (e >> 1), "yl": d["yl"] ^ (e & 1)})


def from_c(value):
    return move(value, ("c",), lambda d: {"c": d["c"] ^ 1})


def ring_pieces(value):
    return [value] + [from_z(value, k) for k in (1, 2, 3)]


def add_low(left, right):
    return (left.astype(F32) + right.astype(F32)).astype(BF)


def ring_sum(p0, p1, p2, p3):
    got = [from_z(p2, 2), from_z(p1, 3), from_z(p3, 1)]
    return sum((v.astype(F32) for v in got), p0.astype(F32))


def rows_of(whole, k, rows):
    z = lax.axis_index("z")
    return lax.dynamic_slice_in_dim(whole, ((z + k) % 4) * rows, rows, 0)


def tie(*values):
    return lax.optimization_barrier(values)


PLANE = ("yh", "x", "c", "yl")
DP = ("yh", "x", "c")
SEQ = ("yl", "z")


def one_way(value, k, along_x, send):
    def source(d):
        if d["c"] in along_x:
            return dict(d, x=d["x"] + (4 - k if send else k))
        return dict(d, yh=d["yh"] ^ (k >> 1), yl=d["yl"] ^ (k & 1))

    return move(value, PLANE, source)


def gather_near(value):
    return jnp.stack([value] + [one_way(value, k, (0,), False) for k in (1, 2, 3)])


def gather_far(near):
    return [near] + [one_way(near, k, (1,), False) for k in (1, 2, 3)]


def sum_far(terms):
    total = terms[0].astype(F32)
    for k in (1, 2, 3):
        total = total + one_way(terms[k], k, (1,), True).astype(F32)
    return total.astype(BF)


def sum_near(low):
    total = low[0].astype(F32)
    for k in (1, 2, 3):
        total = total + one_way(low[k], k, (0,), True).astype(F32)
    return total


def by_core(first, second):
    c = lax.axis_index("c")
    return jnp.where(c == 0, first, second), jnp.where(c == 0, second, first)


def doc_layout(lengths, token_count):
    ends = jnp.cumsum(lengths)
    starts = ends - lengths
    places = jnp.arange(token_count, dtype=jnp.int32)
    inside = (places[:, None] >= starts[None, :]) & (places[:, None] < ends[None, :])
    labels = jnp.arange(lengths.shape[0], dtype=jnp.int32)
    segment = jnp.sum(jnp.where(inside, labels[None, :], 0), axis=1)
    offset = places - jnp.sum(jnp.where(inside, starts[None, :], 0), axis=1)
    return (places, segment, offset)


def rope_tables(offset, half_dim):
    freqs = THETA ** (-jnp.arange(half_dim, dtype=F32) * 2.0 / (2.0 * half_dim))
    angles = offset.astype(F32)[:, None] * freqs[None, :]
    return (jnp.cos(angles), jnp.sin(angles))


def rotate(values, cos_table, sine_table):
    half_dim = values.shape[-1] // 2
    left_half = values[..., :half_dim]
    right_half = values[..., half_dim:]
    return jnp.concatenate(
        [
            left_half * cos_table - right_half * sine_table,
            left_half * sine_table + right_half * cos_table,
        ],
        axis=-1,
    )


def rms_scale(values):
    return lax.rsqrt(jnp.mean(values * values, axis=-1, keepdims=True) + EPS)


def norm_back(grad_normed, unit_rows, scale_rows, gain_row):
    scaled = grad_normed * gain_row
    return scale_rows * (scaled - unit_rows * jnp.mean(scaled * unit_rows, axis=-1, keepdims=True))


def adamw_step(weight, moment, squares, grad, rate, decay):
    moment_new = BETA_ONE * moment + (1.0 - BETA_ONE) * grad
    squares_new = BETA_TWO * squares + (1.0 - BETA_TWO) * grad * grad
    first_fix = 1.0 - BETA_ONE**STEP
    second_fix = 1.0 - BETA_TWO**STEP
    update = moment_new / first_fix / (jnp.sqrt(squares_new / second_fix) + ADAM_EPS)
    master = weight - rate * (update + decay * weight)
    return (moment_new, squares_new, master)


def full_step(weight, moment, squares, average, grad, rate, decay):
    keep = min(0.999, (1.0 + STEP) / (10.0 + STEP))
    moment_new, squares_new, master = adamw_step(weight, moment, squares, grad, rate, decay)
    return (grad, moment_new, squares_new, master, keep * average + (1.0 - keep) * master)


def mm(left, right):
    return jnp.dot(left, right, preferred_element_type=F32)


def mm_nt(left, right):
    return lax.dot_general(left, right, (((1,), (1,)), ((), ())), preferred_element_type=F32)


def mm_tn(left, right):
    return lax.dot_general(left, right, (((0,), (0,)), ((), ())), preferred_element_type=F32)


VMEM_SPEC = pl.BlockSpec(memory_space=pltpu.VMEM)
SMEM_SPEC = pl.BlockSpec(memory_space=pltpu.SMEM)
ANY_SPEC = pl.BlockSpec(memory_space=pl.ANY)
BIG = pltpu.CompilerParams(vmem_limit_bytes=56 * 1024 * 1024)


def shape(dims, dtype):
    return jax.ShapeDtypeStruct(dims, dtype)


def lanes(ref, block, wide):
    return ref[:, pl.ds(pl.multiple_of(block * wide, wide), wide)]


def pair_at(place, dyh, dx):
    return (place[0] ^ dyh) * 4 + ((place[1] + dx) & 3)


def att_weights_kernel(place, *refs):
    blocks, out_w, query_w, sems = refs[:8], refs[8], refs[9], refs[10]
    cols = blocks[0].shape[2]
    out_rows, query_rows = out_w.shape[1] // 8, query_w.shape[1] // 8
    copies = []
    for other in (0, 1):
        half = place[2] ^ other
        col = pl.ds(pl.multiple_of(half * cols, cols), cols)
        for j in range(4):
            for i in range(4):
                dx = jnp.where(half == 0, i, j)
                e = jnp.where(half == 0, j, i)
                pair = pair_at(place, e >> 1, dx)
                src = blocks[4 * other + j].at[i]
                row = pl.ds(pl.multiple_of(pair * out_rows, out_rows), out_rows)
                copies.append((src.at[pl.ds(0, out_rows)], out_w.at[e & 1, row, col]))
                row = pl.ds(pl.multiple_of(pair * query_rows, query_rows), query_rows)
                copies.append((src.at[pl.ds(out_rows, query_rows)], query_w.at[e & 1, row, col]))
    copies = [pltpu.make_async_copy(a, b, sems.at[n]) for n, (a, b) in enumerate(copies)]
    for copy in copies:
        copy.start()
    for copy in copies:
        copy.wait()


def att_weights(place, blocks):
    rows, cols = blocks[0].shape[1:]
    return pl.pallas_call(
        att_weights_kernel,
        in_specs=[SMEM_SPEC] + [ANY_SPEC] * 8,
        out_specs=[VMEM_SPEC] * 2,
        out_shape=[shape((2, 8 * (rows // 3 * 2), 2 * cols), BF), shape((2, 8 * (rows // 3), 2 * cols), BF)],
        scratch_shapes=[pltpu.SemaphoreType.DMA((64,))],
        compiler_params=BIG,
    )(place, *blocks)


def place_rows_kernel(first, *refs):
    out = refs[-1]
    rows = refs[0].shape[0]
    for k, piece in enumerate(refs[:-1]):
        at = ((first[0] + k) & 3) * rows
        out[pl.ds(pl.multiple_of(at, rows), rows)] = piece[...]


def place_rows(pieces, first):
    rows, cols = pieces[0].shape
    return pl.pallas_call(
        place_rows_kernel,
        in_specs=[SMEM_SPEC] + [VMEM_SPEC] * 4,
        out_specs=VMEM_SPEC,
        out_shape=shape((4 * rows, cols), pieces[0].dtype),
        compiler_params=BIG,
    )(first, *pieces)


def project_kernel(first, p0, p1, p2, p3, gain, cos_ref, sine_ref, nq, kv, latent_own, whole):
    cols = p0.shape[1]
    for k, piece in enumerate((p0, p1, p2, p3)):
        at = ((first[0] + k) & 3) * cols
        whole[:, pl.ds(pl.multiple_of(at, cols), cols)] = piece[...]
    latent = whole[:, :QLAT].astype(F32)
    nq[...] = (latent * rms_scale(latent) * gain[...]).astype(BF)
    keys = whole[:, QLAT : QLAT + HDIM].astype(F32)
    kv[:, :HDIM] = turn(keys, cos_ref[...], sine_ref[...]).astype(BF)
    kv[:, HDIM:] = whole[:, QLAT + HDIM :]
    rows = latent_own.shape[0]
    latent_own[...] = whole[pl.ds(pl.multiple_of(first[0] * rows, rows), rows), :QLAT]


def project(first, pieces, gain, cos_table, sine_table):
    line, cols = pieces[0].shape
    return pl.pallas_call(
        project_kernel,
        in_specs=[SMEM_SPEC] + [VMEM_SPEC] * 7,
        out_specs=[VMEM_SPEC] * 3,
        out_shape=[shape((line, QLAT), BF), shape((line, 2 * HDIM), BF), shape((line // 4, QLAT), BF)],
        scratch_shapes=[pltpu.VMEM((line, 4 * cols), BF)],
        compiler_params=BIG,
    )(first, *pieces, gain, cos_table, sine_table)


def hidden_kernel(place, n2, back, blocks, grads, hidden, turned, gate_up, down, weights, sems, out_sems):
    half_cols, wide = blocks.shape[2] // 2, blocks.shape[3]
    count = weights.shape[1]
    copies = [[], []]
    for half in (0, 1):
        for slot in (0, 1):
            for d in range(blocks.shape[0] // 2):
                src = blocks.at[2 * d + (place[3] ^ slot), :, pl.ds(half * half_cols, half_cols)]
                row = (2 * half + slot) * half_cols
                dst = weights.at[:, pl.ds(row, half_cols), pl.ds(d * wide, wide)]
                at = half * 32 + len(copies[half])
                copies[half].append(pltpu.make_async_copy(src, dst, sems.at[at]))
    for copy in copies[0] + copies[1]:
        copy.start()
    outs = []
    for half in (0, 1):
        rows = pl.ds(half * 2 * half_cols, 2 * half_cols)
        outs.append(
            [
                pltpu.make_async_copy(weights.at[:2, rows], gate_up.at[:, rows], out_sems.at[2 * half]),
                pltpu.make_async_copy(weights.at[2, rows], down.at[rows], out_sems.at[2 * half + 1]),
            ]
        )

    def ready(half):
        for copy in copies[half]:
            copy.wait()
        for copy in outs[half]:
            copy.start()

    ready(0)
    for start in range(0, count, 256):
        size = min(256, count - start)
        if start <= 2 * half_cols < start + size:
            ready(1)
        rows = pl.ds(start, size)
        gate = mm_nt(n2[...], weights[0, rows])
        up = mm_nt(n2[...], weights[1, rows])
        grad = mm_nt(back[...], weights[2, rows])
        s = jax.nn.sigmoid(gate)
        silu = gate * s
        parts = [
            (grad * up * s * (1.0 + gate * (1.0 - s))).astype(BF),
            (grad * silu).astype(BF),
            (silu * up).astype(BF),
        ]
        grads[:, rows] = parts[0]
        grads[:, pl.ds(count + start, size)] = parts[1]
        hidden[:, rows] = parts[2]
        for m, part in enumerate(parts):
            turned[m, rows] = part.T
    for copy in outs[0] + outs[1]:
        copy.wait()


def hidden_units(place, n2_rows, back_rows, blocks):
    line = n2_rows.shape[0]
    cols, wide = blocks.shape[2:]
    whole = blocks.shape[0] // 2 * wide
    return pl.pallas_call(
        hidden_kernel,
        in_specs=[SMEM_SPEC] + [VMEM_SPEC] * 2 + [ANY_SPEC],
        out_specs=[VMEM_SPEC] * 3 + [ANY_SPEC] * 2,
        out_shape=[
            shape((line, 4 * cols), BF),
            shape((line, 2 * cols), BF),
            shape((3, 2 * cols, line), BF),
            shape((2, 2 * cols, whole), BF),
            shape((2 * cols, whole), BF),
        ],
        scratch_shapes=[
            pltpu.VMEM((3, 2 * cols, whole), BF),
            pltpu.SemaphoreType.DMA((64,)),
            pltpu.SemaphoreType.DMA((4,)),
        ],
        compiler_params=BIG,
    )(place, n2_rows, back_rows, blocks)


def spot(place, slot, step):
    e = 2 * (step >> 2) + slot
    dx = step & 3
    first = place[2] == 0
    return jnp.where(first, e, dx), jnp.where(first, dx, e)


def hidden_grads_kernel(place, own, other, n2_own, n2_other, back_own, back_other, dst, buf, sems):
    mat, step = pl.program_id(0), pl.program_id(1)
    at = mat * pl.num_programs(1) + step
    turn_of = lax.rem(at, 2)
    wide = dst.shape[5]
    rows = dst.shape[4]
    pair = pair_at(place, step >> 2, step & 3)

    def copies():
        made = []
        for slot in (0, 1):
            i, j = spot(place, slot, step)
            made.append(
                pltpu.make_async_copy(buf.at[turn_of, slot], dst.at[i, j, :, mat], sems.at[turn_of, slot])
            )
        return made

    @pl.when(at >= 2)
    def _():
        for copy in copies():
            copy.wait()

    def put(rows_own, rows_other):
        terms = mm(own[0], lanes(rows_own, pair, 2 * wide)) + mm(other[0], lanes(rows_other, pair, 2 * wide))
        terms = terms.astype(BF)
        for slot in (0, 1):
            for k in (0, 1):
                buf[turn_of, slot, k] = terms[slot * rows : (slot + 1) * rows, k * wide : (k + 1) * wide]

    @pl.when(mat < 2)
    def _():
        put(n2_own, n2_other)

    @pl.when(mat == 2)
    def _():
        put(back_own, back_other)

    for copy in copies():
        copy.start()

    @pl.when(at == pl.num_programs(0) * pl.num_programs(1) - 1)
    def _():
        for copy in copies():
            copy.wait()
        for slot in (0, 1):
            pltpu.make_async_copy(
                buf.at[1 - turn_of, slot], dst.at[0, 0, :, mat], sems.at[1 - turn_of, slot]
            ).wait()


def hidden_grads(place, own, other, n2_own, n2_other, back_own, back_other):
    count, line = own.shape[1:]
    cols = count // 2
    wide = n2_own.shape[1] // 16
    units_spec = pl.BlockSpec((1, cols, line), lambda m, t, place: (m, place[2], 0))
    rows_spec = pl.BlockSpec(n2_own.shape, lambda m, t, place: (0, 0))
    return pl.pallas_call(
        hidden_grads_kernel,
        grid_spec=pltpu.PrefetchScalarGridSpec(
            num_scalar_prefetch=1,
            grid=(3, 8),
            in_specs=[units_spec] * 2 + [rows_spec] * 4,
            out_specs=ANY_SPEC,
            scratch_shapes=[
                pltpu.VMEM((2, 2, 2, cols // 2, wide), BF),
                pltpu.SemaphoreType.DMA((2, 2)),
            ],
        ),
        out_shape=shape((4, 4, 2, 3, cols // 2, wide), BF),
        compiler_params=BIG,
    )(place, own, other, n2_own, n2_other, back_own, back_other)


def att_grads_kernel(place, dh_own, dh_other, nq_own, nq_other, a_own, a_other, g_own, g_other, dst):
    rows = 2 * dh_own.shape[1] // 2
    both = lambda a, b: jnp.concatenate([a[...], b[...]], axis=0)
    dst[0, 0, :rows] = mm_tn(both(dh_own, dh_other), both(a_own, a_other)).astype(BF)
    dst[0, 0, rows:] = mm_tn(both(nq_own, nq_other), both(g_own, g_other)).astype(BF)


def att_grads(place, dh, nq, attended, grad_pre):
    line = dh[0].shape[0]
    out_rows, query_rows = dh[0].shape[1] // 8, nq[0].shape[1] // 8
    cols = attended[0].shape[1] // 4
    pair = lambda wide: pl.BlockSpec((line, wide), lambda s, t, place: (0, pair_at(place, t >> 2, t & 3)))
    half = pl.BlockSpec((line, cols), lambda s, t, place: (0, 2 * s + place[2]))
    return pl.pallas_call(
        att_grads_kernel,
        grid_spec=pltpu.PrefetchScalarGridSpec(
            num_scalar_prefetch=1,
            grid=(2, 8),
            in_specs=[pair(out_rows)] * 2 + [pair(query_rows)] * 2 + [half] * 4,
            out_specs=pl.BlockSpec(
                (1, 1, out_rows + query_rows, cols), lambda s, t, place: spot(place, s, t) + (0, 0)
            ),
        ),
        out_shape=shape((4, 4, out_rows + query_rows, cols), BF),
        compiler_params=BIG,
    )(place, *dh, *nq, *attended, *grad_pre)


def entry_kernel(place, rows, own, other, out):
    total = 0.0
    wide = own.shape[2]
    for dc, buf in enumerate((own, other)):
        for dx in range(4):
            left = [
                lanes(rows, pair_at(place, dyh, dx) * 2 + (place[2] ^ dc), wide) for dyh in (0, 1)
            ]
            total = total + mm(jnp.concatenate(left, axis=1), buf[dx].reshape(2 * wide, -1))
    out[...] = total.astype(BF)


def entry_project(place, rows, own, other):
    return pl.pallas_call(
        entry_kernel,
        in_specs=[SMEM_SPEC] + [VMEM_SPEC] * 3,
        out_specs=VMEM_SPEC,
        out_shape=shape((rows.shape[0], own.shape[3]), BF),
        compiler_params=BIG,
    )(place, rows, own, other)


def entry_grads_kernel(place, n1_own, n1_other, df_own, df_other, dst):
    wide = dst.shape[2]
    right = jnp.concatenate([df_own[...], df_other[...]], axis=0)
    for dyh in (0, 1):
        for dx in range(4):
            block = pair_at(place, dyh, dx) * 2 + place[2]
            left = jnp.concatenate([lanes(n1_own, block, wide), lanes(n1_other, block, wide)], axis=0)
            dst[dyh, dx] = mm_tn(left, right).astype(BF)


def entry_grads(place, n1_own, n1_other, df_own, df_other):
    return pl.pallas_call(
        entry_grads_kernel,
        in_specs=[SMEM_SPEC] + [VMEM_SPEC] * 4,
        out_specs=VMEM_SPEC,
        out_shape=shape((2, 4, n1_own.shape[1] // 16, df_own.shape[1]), BF),
        compiler_params=BIG,
    )(place, n1_own, n1_other, df_own, df_other)


def finish_kernel(grad_first, whole, x_ref, mid_ref, gain_ref, grad_out, gain_row):
    grad = mm_nt(grad_first[...], whole[...])
    x = x_ref[...].astype(F32)
    scale = rms_scale(x)
    unit = x * scale
    gain_row[...] = jnp.sum(grad * unit, axis=0, keepdims=True)
    grad_out[...] = mid_ref[...] + norm_back(grad, unit, scale, gain_ref[...])


def finish(grad_first, whole, tokens, grad_middle, gain_one):
    rows = tokens.shape[0]
    return pl.pallas_call(
        finish_kernel,
        in_specs=[VMEM_SPEC] * 5,
        out_specs=[VMEM_SPEC] * 2,
        out_shape=[shape((rows, D), F32), shape((1, D), F32)],
        compiler_params=BIG,
    )(grad_first, whole, tokens, grad_middle, gain_one)


def turn(values, cos_table, sine_table):
    half = values.shape[1] // 2
    left, right = values[:, :half], values[:, half:]
    return jnp.concatenate(
        [left * cos_table - right * sine_table, left * sine_table + right * cos_table], axis=1
    )


def attend_kernel(info, pre, kv_own, kv_other, starts, cos_ref, sine_ref, q_out, out, w_own, w_other):
    yl = info[0]
    line = pre.shape[0]
    block = 128
    queries = turn(pre[...], cos_ref[...], sine_ref[...]).astype(BF)
    q_out[...] = queries
    scale = HDIM ** (-0.5)

    def work(with_other):
        for at in range(0, line, block):
            end = at + block
            q = queries[at:end]
            first = starts[at:end] - yl * line
            own = mm_nt(q, kv_own[:end, :HDIM]) * scale
            spot = lax.broadcasted_iota(jnp.int32, (block, end), 1)
            row = at + lax.broadcasted_iota(jnp.int32, (block, end), 0)
            own = jnp.where((spot <= row) & (spot >= first), own, MASKED)
            top = jnp.max(own, axis=1, keepdims=True)
            if with_other:
                far = mm_nt(q, kv_other[:, :HDIM]) * scale
                far_spot = lax.broadcasted_iota(jnp.int32, (block, line), 1) - line
                far = jnp.where(far_spot >= first, far, MASKED)
                top = jnp.maximum(top, jnp.max(far, axis=1, keepdims=True))
                far = jnp.exp(far - top)
            own = jnp.exp(own - top)
            total = jnp.sum(own, axis=1, keepdims=True)
            if with_other:
                total = total + jnp.sum(far, axis=1, keepdims=True)
            share = 1.0 / total
            own = (own * share).astype(BF)
            w_own[0, at:end, :end] = own
            if end < line:
                w_own[0, at:end, end:] = jnp.zeros((block, line - end), BF)
            result = mm(own, kv_own[:end, HDIM:])
            if with_other:
                far = (far * share).astype(BF)
                w_other[0, at:end] = far
                result = result + mm(far, kv_other[:, HDIM:])
            out[at:end] = result.astype(BF)

    @pl.when(yl == 0)
    def _():
        work(False)

    @pl.when(yl == 1)
    def _():
        work(True)


def attend(info, pre, kv_own, kv_other, starts, cos_table, sine_table):
    line, width = pre.shape
    heads = width // HDIM
    whole = lambda v: pl.BlockSpec(v.shape, lambda h: (0, 0))
    head = pl.BlockSpec((line, HDIM), lambda h: (0, h))
    weights = pl.BlockSpec((1, line, line), lambda h: (h, 0, 0))
    return pl.pallas_call(
        attend_kernel,
        grid=(heads,),
        in_specs=[SMEM_SPEC, head]
        + [whole(v) for v in (kv_own, kv_other, starts, cos_table, sine_table)],
        out_specs=[head, head, weights, weights],
        out_shape=[shape((line, width), BF)] * 2 + [shape((heads, line, line), BF)] * 2,
        compiler_params=BIG,
    )(info, pre, kv_own, kv_other, starts, cos_table, sine_table)


def attend_back_kernel(
    info, grad_out, out, queries, kv_own, kv_other, w_own, w_other, cos_ref, sine_ref,
    grad_q, grad_kv, scores, k_own, v_own, k_far, v_far,
):
    yl = info[0]
    head = pl.program_id(0)
    line = queries.shape[0]
    block = 128
    scale = HDIM ** (-0.5)

    @pl.when(head == 0)
    def _():
        for ref in (k_own, v_own, k_far, v_far):
            ref[...] = jnp.zeros_like(ref)

    g = grad_out[...]
    delta = jnp.sum(g.astype(F32) * out[...].astype(F32), axis=1, keepdims=True)

    def work(with_other):
        for at in range(0, line, block):
            end = at + block
            own = mm_nt(g[at:end], kv_own[:end, HDIM:]) - delta[at:end]
            own = (w_own[0, at:end, :end].astype(F32) * own).astype(BF)
            scores[at:end, :end] = own
            grad = mm(own, kv_own[:end, :HDIM])
            if with_other:
                far = mm_nt(g[at:end], kv_other[:, HDIM:]) - delta[at:end]
                far = (w_other[0, at:end].astype(F32) * far).astype(BF)
                scores[at:end, line:] = far
                grad = grad + mm(far, kv_other[:, :HDIM])
            grad_q[at:end] = turn(grad * scale, cos_ref[at:end], -sine_ref[at:end]).astype(BF)
        for at in range(0, line, block):
            end = at + block
            k_own[at:end] += mm_tn(scores[at:, at:end], queries[at:])
            v_own[at:end] += mm_tn(w_own[0, at:, at:end], g[at:])
        if with_other:
            k_far[...] += mm_tn(scores[:, line:], queries[...])
            v_far[...] += mm_tn(w_other[0], g)

    @pl.when(yl == 0)
    def _():
        work(False)

    @pl.when(yl == 1)
    def _():
        work(True)

    @pl.when(head == pl.num_programs(0) - 1)
    def _():
        for i, (ref, factor) in enumerate(((k_own, scale), (v_own, 1.0), (k_far, scale), (v_far, 1.0))):
            grad_kv[:, i * HDIM : (i + 1) * HDIM] = (ref[...] * factor).astype(BF)


def attend_back(info, grad_out, out, queries, kv_own, kv_other, w_own, w_other, cos_table, sine_table):
    line, width = queries.shape
    heads = width // HDIM
    whole = lambda v: pl.BlockSpec(v.shape, lambda h: (0, 0))
    head = pl.BlockSpec((line, HDIM), lambda h: (0, h))
    weights = pl.BlockSpec((1, line, line), lambda h: (h, 0, 0))
    return pl.pallas_call(
        attend_back_kernel,
        grid=(heads,),
        in_specs=[SMEM_SPEC, head, head, head, whole(kv_own), whole(kv_other), weights, weights]
        + [whole(cos_table), whole(sine_table)],
        out_specs=[head, pl.BlockSpec((line, 4 * HDIM), lambda h: (0, 0))],
        out_shape=[shape((line, width), BF), shape((line, 4 * HDIM), BF)],
        scratch_shapes=[pltpu.VMEM((line, 2 * line), BF)] + [pltpu.VMEM((line, HDIM), F32)] * 4,
        compiler_params=BIG,
    )(info, grad_out, out, queries, kv_own, kv_other, w_own, w_other, cos_table, sine_table)


def local(
    tokens,
    cotangent,
    doc_lengths,
    entry_weight,
    entry_first,
    entry_second,
    entry_average,
    query_weight,
    query_first,
    query_second,
    query_average,
    out_weight,
    out_first,
    out_second,
    out_average,
    ffn_weight,
    ffn_first,
    ffn_second,
    ffn_average,
    norm_gains,
    gains_first,
    gains_second,
    gains_average,
):
    rows = tokens.shape[0]
    line = 4 * rows
    z, yl, c = lax.axis_index("z"), lax.axis_index("yl"), lax.axis_index("c")
    place = jnp.stack([lax.axis_index(a) for a in ("yh", "x", "c", "yl")]).astype(jnp.int32)
    wide = D // 16
    ffn_cols = ffn_weight.shape[2]
    half_cols = ffn_cols // 2
    entry_cols = entry_weight.shape[1]
    slot_cols = entry_cols // 4
    head_cols = query_weight.shape[1]
    gain_one = 1.0 + norm_gains[None, :D]
    gain_query = 1.0 + norm_gains[D : D + QLAT]
    gain_two = 1.0 + norm_gains[None, D + QLAT :]

    ffn_low = jnp.transpose(ffn_weight, (1, 2, 0)).astype(BF)
    ffn_all = lax.all_gather(ffn_low, PLANE, axis=0, tiled=False)

    inputs = tokens.astype(F32)
    scale_one = rms_scale(inputs)
    normed_one = (inputs * scale_one * gain_one).astype(BF)
    first = z[None].astype(jnp.int32)
    start = jnp.zeros((1,), jnp.int32)
    n1_rows = place_rows(ring_pieces(normed_one), first)

    entry_low = entry_weight.astype(BF)
    slot = lax.dynamic_slice_in_dim(entry_low, z * slot_cols, slot_cols, 1)
    slot = jnp.stack([slot, from_y(slot, 3)])
    slot = jnp.stack([slot] + [from_x(slot, k) for k in (1, 2, 3)])
    slot_other = from_c(slot)

    att_half = head_cols // 2
    out_late, query_late, slot = tie(out_weight, query_weight, slot)
    halves = [
        (out_late[:, h * att_half : (h + 1) * att_half], query_late[:, h * att_half : (h + 1) * att_half])
        for h in (0, 1)
    ]
    keep, give = by_core(*[jnp.concatenate(h, axis=0).astype(BF) for h in halves])
    got = from_c(give)
    att_0, att_1 = by_core(keep, got)
    att_own = jnp.concatenate([att_0[:wide], att_1[:wide], att_0[wide:], att_1[wide:]], axis=0)
    att_near = gather_near(att_own)

    f_slot = entry_project(place, n1_rows, slot, slot_other)
    f_slot, att_near, doc_lengths, cot_late = tie(f_slot, att_near, doc_lengths, cotangent)
    att_far = gather_far(att_near)
    out_low, query_low = att_weights(place, att_far + [from_c(v) for v in att_far])
    places_all, segment_all, offset_all = doc_layout(doc_lengths[0], 2 * line)
    line_offset = lax.dynamic_slice_in_dim(offset_all, yl * line, line)
    line_places = yl * line + jnp.arange(line, dtype=jnp.int32)
    starts = (line_places - line_offset)[:, None]
    cos_line, sine_line = rope_tables(line_offset, HDIM // 2)
    query_rows, kv_own, latent_own = project(
        first, ring_pieces(f_slot), gain_query[None], cos_line, sine_line
    )
    kv_other = from_y(kv_own, 1)
    info = place[3:]
    pre = jnp.concatenate([mm(query_rows, query_low[s]) for s in (0, 1)], axis=1)
    queries, attended, w_own, w_other = attend(
        info, pre, kv_own, kv_other, starts, cos_line, sine_line
    )

    back_rows = place_rows(ring_pieces(cot_late), start)
    attended, back_rows = tie(attended, back_rows)
    branch = sum(mm_nt(attended[:, s * head_cols : (s + 1) * head_cols], out_low[s]) for s in (0, 1)).astype(BF)
    middle = inputs + ring_sum(*[rows_of(branch, k, rows) for k in range(4)])
    scale_two = rms_scale(middle)
    unit_two = middle * scale_two
    normed_two = (unit_two * gain_two).astype(BF)

    n2_rows = place_rows(ring_pieces(normed_two), start)
    units, hidden_low, turned, gate_up_low, down_low = hidden_units(place, n2_rows, back_rows, ffn_all)
    n2_part = mm(units, gate_up_low.reshape(-1, D)).astype(BF)
    mixed_part = mm(hidden_low, down_low).astype(BF)
    grad_normed_two = ring_sum(*[n2_part[k * rows : (k + 1) * rows] for k in range(4)])
    mixed = middle + ring_sum(*[mixed_part[k * rows : (k + 1) * rows] for k in range(4)])
    mixed_out = mixed.astype(BF)
    grad_middle = cotangent.astype(F32) + norm_back(grad_normed_two, unit_two, scale_two, gain_two)
    dh_rows = place_rows(ring_pieces(grad_middle.astype(BF)), first)

    ffn_terms = hidden_grads(
        place, turned, from_c(turned), n2_rows, from_c(n2_rows), back_rows, from_c(back_rows)
    )
    dh_rows, ffn_terms = tie(dh_rows, ffn_terms)
    ffn_far = sum_far(ffn_terms)

    grad_attended = jnp.concatenate([mm(dh_rows, out_low[s]).astype(BF) for s in (0, 1)], axis=1)
    grad_query_pre, grad_kv = attend_back(
        info, grad_attended, attended, queries, kv_own, kv_other, w_own, w_other, cos_line, sine_line
    )
    grad_nq = sum(
        mm_nt(grad_query_pre[:, s * head_cols : (s + 1) * head_cols], query_low[s]) for s in (0, 1)
    ).astype(BF)
    sums = jnp.concatenate([grad_nq, grad_kv], axis=1)
    summed = ring_sum(*[rows_of(sums, k, rows) for k in range(4)])
    pair = lambda v: (v, from_c(v))
    att_terms = att_grads(place, pair(dh_rows), pair(query_rows), pair(attended), pair(grad_query_pre))
    summed, att_terms, ffn_far = tie(summed, att_terms, ffn_far)
    att_sums = sum_far(att_terms)
    grad_normed_query = summed[:, :QLAT]
    kv_grad = summed[:, QLAT : QLAT + 2 * HDIM] + from_y(
        summed[:, QLAT + 2 * HDIM :].astype(BF), 1
    ).astype(F32)
    own = lambda v: rows_of(v, 0, rows)
    latent = latent_own.astype(F32)
    scale_query = rms_scale(latent)
    unit_query = latent * scale_query
    grad_latent = norm_back(grad_normed_query, unit_query, scale_query, gain_query)
    grad_first = jnp.concatenate(
        [grad_latent, rotate(kv_grad[:, :HDIM], own(cos_line), -own(sine_line)), kv_grad[:, HDIM:]], axis=1
    ).astype(BF)

    entry_low, _ = tie(entry_low, units)
    entry_all = lax.all_gather(entry_low, DP, axis=0, tiled=True)
    grad_first, att_sums = tie(grad_first, att_sums)
    input_grad, one_row = finish(grad_first, entry_all, tokens, grad_middle, gain_one)

    att_got = sum_near(att_sums)
    ffn_got = sum_near(ffn_far)

    def own_halves(got_0, got_1):
        mine, theirs = by_core(got_0, got_1)
        return by_core(mine, from_c(theirs.astype(BF)).astype(F32))

    att_grad = own_halves(
        jnp.concatenate([att_got[:wide], att_got[2 * wide : 5 * wide // 2]], axis=0),
        jnp.concatenate([att_got[wide : 2 * wide], att_got[5 * wide // 2 :]], axis=0),
    )
    att_grad = jnp.concatenate(att_grad, axis=1)
    out_grad, query_grad = att_grad[:wide], att_grad[wide:]
    ffn_grad = jnp.transpose(jnp.concatenate(own_halves(ffn_got[0], ffn_got[1]), axis=1), (2, 0, 1))

    gain_terms = jnp.concatenate(
        [
            one_row[0],
            jnp.sum(grad_normed_query * unit_query, axis=0),
            jnp.sum(grad_normed_two * unit_two, axis=0),
        ]
    )
    gain_count = gain_terms.shape[0]
    gain_height = -(-gain_count // (16 * slot_cols)) * 16

    def with_gains(value, gains):
        padded = jnp.pad(gains, (0, gain_height * slot_cols - gain_count))
        return jnp.concatenate([value, padded.reshape(gain_height, slot_cols).astype(BF)], axis=0)

    def split_gains(message):
        got = message[-gain_height:].astype(F32).reshape(-1)[:gain_count]
        return message[:-gain_height], got

    def exchange(values, moves, gains):
        sent = [split_gains(step(with_gains(v, gains))) for v, step in zip(values, moves)]
        return [v for v, _ in sent], gains + sum(g for _, g in sent)

    cols_of = lambda k: lax.dynamic_slice_in_dim(grad_first, ((z + k) % 4) * slot_cols, slot_cols, 1)
    df_slot = place_rows([cols_of(0)] + [from_z(cols_of(4 - k), k) for k in (1, 2, 3)], first)
    (df_other,), gains_grad = exchange([df_slot], [from_c], gain_terms)
    entry_terms = entry_grads(place, n1_rows, from_c(n1_rows), df_slot, df_other)
    got, gains_grad = exchange(
        [entry_terms[:, k].reshape(2 * wide, slot_cols) for k in (1, 2, 3)],
        [lambda v, k=k: from_x(v, 4 - k) for k in (1, 2, 3)],
        gains_grad,
    )
    part = sum((v.astype(F32) for v in got), entry_terms[:, 0].reshape(2 * wide, slot_cols).astype(F32))
    low = part.astype(BF).reshape(2, wide, slot_cols)
    got, gains_grad = exchange(
        [low[e >> 1] for e in (1, 2, 3)], [lambda v, e=e: from_y(v, e) for e in (1, 2, 3)], gains_grad
    )
    low = sum((v.astype(F32) for v in got), part[:wide]).astype(BF)
    got, gains_grad = exchange(
        [low] * 3, [lambda v, k=k: from_z(v, k) for k in (1, 2, 3)], gains_grad
    )
    entry_grad = jnp.zeros((wide, entry_cols), BF)
    for k, piece in enumerate([low] + got):
        entry_grad = lax.dynamic_update_slice_in_dim(entry_grad, piece, ((z + k) % 4) * slot_cols, 1)
    entry_grad = entry_grad.astype(F32)

    return (
        (mixed_out, input_grad)
        + full_step(entry_weight, entry_first, entry_second, entry_average, entry_grad, ENTRY_RATE, DECAY)
        + full_step(query_weight, query_first, query_second, query_average, query_grad, QUERY_RATE, DECAY)
        + full_step(out_weight, out_first, out_second, out_average, out_grad, OUT_RATE, DECAY)
        + full_step(ffn_weight, ffn_first, ffn_second, ffn_average, ffn_grad, FFN_RATE, DECAY)
        + full_step(norm_gains, gains_first, gains_second, gains_average, gains_grad, GAIN_RATE, 0.0)
    )


def solution(mesh):
    fine = Mesh(mesh.devices.reshape(tuple(SIZES[a] for a in AXES)), AXES)
    tokens = P(AXES, None)
    entry = P(DP, None)
    middle = P(DP, SEQ)
    ffn = P(DP, None, SEQ)
    gains = P()
    return jax.shard_map(
        local,
        mesh=fine,
        in_specs=(tokens, tokens, entry) + (entry,) * 4 + (middle,) * 8 + (ffn,) * 4 + (gains,) * 4,
        out_specs=(tokens, tokens) + (entry,) * 5 + (middle,) * 10 + (ffn,) * 5 + (gains,) * 5,
        check_vma=False,
    )
```

```python
import functools

import jax
import jax.numpy as jnp
import numpy as np
from jax import lax
from jax.experimental import pallas as pl
from jax.experimental.pallas import tpu as pltpu
from jax.sharding import Mesh, PartitionSpec as P

D = 2048
QLAT = 1024
HDIM = 256
STEP = 10
EPS = 1e-05
THETA = 10000.0
BETA_ONE = 0.9
BETA_TWO = 0.95
ADAM_EPS = 1e-08
ENTRY_RATE = 0.03
QUERY_RATE = 0.04
OUT_RATE = 0.08
FFN_RATE = 0.03
GAIN_RATE = 0.1
DECAY = 0.1
MASKED = -1e30
SIZES = {"yh": 2, "x": 4, "c": 2, "yl": 2, "z": 4}
AXES = ("yh", "x", "c", "yl", "z")
BF = jnp.bfloat16
F32 = jnp.float32


def move(value, axes, source):
    dims = [SIZES[a] for a in axes]
    pairs = []
    for place in np.ndindex(*dims):
        src = source(dict(zip(axes, place)))
        src_place = [src[a] % SIZES[a] for a in axes]
        pairs.append((int(np.ravel_multi_index(src_place, dims)), int(np.ravel_multi_index(place, dims))))
    return lax.ppermute(value, axes, pairs)


def from_z(value, k):
    return move(value, ("z",), lambda d: {"z": d["z"] + k})


def from_x(value, k):
    return move(value, ("x",), lambda d: {"x": d["x"] + k})


def from_y(value, e):
    return move(value, ("yh", "yl"), lambda d: {"yh": d["yh"] ^ (e >> 1), "yl": d["yl"] ^ (e & 1)})


def from_c(value):
    return move(value, ("c",), lambda d: {"c": d["c"] ^ 1})


def line_pieces(value):
    return [value] + [from_z(value, k) for k in (1, 2, 3)]


def ring_near(value):
    return from_z(value, 1), from_z(value, 3)


def ring_pieces(value, near=None):
    half = value.shape[0] // 2
    after, before = near or ring_near(value)
    top = from_z(after[:half], 1)
    bottom = from_z(before[half:], 3)
    return [value, after, jnp.concatenate([top, bottom], axis=0), before]


def add_low(left, right):
    return (left.astype(F32) + right.astype(F32)).astype(BF)


def total(values):
    return sum((v.astype(F32) for v in values[1:]), values[0].astype(F32))


def line_sum(p0, p1, p2, p3):
    return [p0, from_z(p2, 2), from_z(p1, 3), from_z(p3, 1)]


def ring_sum(p0, p1, p2, p3):
    half = p2.shape[0] // 2
    got_top = from_z(p2[:half], 3)
    got_bottom = from_z(p2[half:], 1)
    p1 = jnp.concatenate([add_low(p1[:half], got_top), p1[half:]], axis=0)
    p3 = jnp.concatenate([p3[:half], add_low(p3[half:], got_bottom)], axis=0)
    return [p0, from_z(p1, 3), from_z(p3, 1)]


def rows_of(whole, k, rows):
    z = lax.axis_index("z")
    return lax.dynamic_slice_in_dim(whole, ((z + k) % 4) * rows, rows, 0)


def tie(*values):
    return lax.optimization_barrier(values)


PLANE = ("yh", "x", "c", "yl")
DP = ("yh", "x", "c")
SEQ = ("yl", "z")


def one_way(value, k, along_x, send):
    def source(d):
        if d["c"] in along_x:
            return dict(d, x=d["x"] + (4 - k if send else k))
        return dict(d, yh=d["yh"] ^ (k >> 1), yl=d["yl"] ^ (k & 1))

    return move(value, PLANE, source)


def gather_near(value):
    return jnp.stack([value] + [one_way(value, k, (0,), False) for k in (1, 2, 3)])


def gather_far(near):
    return [near] + [one_way(near, k, (1,), False) for k in (1, 2, 3)]


def far_moves(terms):
    return [terms[0]] + [one_way(terms[k], k, (1,), True) for k in (1, 3, 2)]


def sum_near(low):
    total = low[0].astype(F32)
    for k in (1, 2, 3):
        total = total + one_way(low[k], k, (0,), True).astype(F32)
    return total


def by_core(first, second):
    c = lax.axis_index("c")
    return jnp.where(c == 0, first, second), jnp.where(c == 0, second, first)


def doc_layout(lengths, token_count):
    ends = jnp.cumsum(lengths)
    starts = ends - lengths
    places = jnp.arange(token_count, dtype=jnp.int32)
    inside = (places[:, None] >= starts[None, :]) & (places[:, None] < ends[None, :])
    labels = jnp.arange(lengths.shape[0], dtype=jnp.int32)
    segment = jnp.sum(jnp.where(inside, labels[None, :], 0), axis=1)
    offset = places - jnp.sum(jnp.where(inside, starts[None, :], 0), axis=1)
    return (places, segment, offset)


def rope_tables(offset, half_dim):
    freqs = THETA ** (-jnp.arange(half_dim, dtype=F32) * 2.0 / (2.0 * half_dim))
    angles = offset.astype(F32)[:, None] * freqs[None, :]
    return (jnp.cos(angles), jnp.sin(angles))


def rotate(values, cos_table, sine_table):
    half_dim = values.shape[-1] // 2
    left_half = values[..., :half_dim]
    right_half = values[..., half_dim:]
    return jnp.concatenate(
        [
            left_half * cos_table - right_half * sine_table,
            left_half * sine_table + right_half * cos_table,
        ],
        axis=-1,
    )


def rms_scale(values):
    return lax.rsqrt(jnp.mean(values * values, axis=-1, keepdims=True) + EPS)


def norm_back(grad_normed, unit_rows, scale_rows, gain_row):
    scaled = grad_normed * gain_row
    return scale_rows * (scaled - unit_rows * jnp.mean(scaled * unit_rows, axis=-1, keepdims=True))


def adamw_step(weight, moment, squares, grad, rate, decay):
    moment_new = BETA_ONE * moment + (1.0 - BETA_ONE) * grad
    squares_new = BETA_TWO * squares + (1.0 - BETA_TWO) * grad * grad
    first_fix = 1.0 - BETA_ONE**STEP
    second_fix = 1.0 - BETA_TWO**STEP
    update = moment_new / first_fix / (jnp.sqrt(squares_new / second_fix) + ADAM_EPS)
    master = weight - rate * (update + decay * weight)
    return (moment_new, squares_new, master)


def full_step(weight, moment, squares, average, grad, rate, decay):
    keep = min(0.999, (1.0 + STEP) / (10.0 + STEP))
    moment_new, squares_new, master = adamw_step(weight, moment, squares, grad, rate, decay)
    return (grad, moment_new, squares_new, master, keep * average + (1.0 - keep) * master)


def mm(left, right):
    return jnp.dot(left, right, preferred_element_type=F32)


def mm_nt(left, right):
    return lax.dot_general(left, right, (((1,), (1,)), ((), ())), preferred_element_type=F32)


def mm_tn(left, right):
    return lax.dot_general(left, right, (((0,), (0,)), ((), ())), preferred_element_type=F32)


VMEM_SPEC = pl.BlockSpec(memory_space=pltpu.VMEM)
SMEM_SPEC = pl.BlockSpec(memory_space=pltpu.SMEM)
ANY_SPEC = pl.BlockSpec(memory_space=pl.ANY)
BIG = pltpu.CompilerParams(vmem_limit_bytes=56 * 1024 * 1024)


def cost(micros):
    return pl.CostEstimate(
        flops=int(micros * 1.1e9), bytes_accessed=int(micros * 3.3e6), transcendentals=0
    )


def shape(dims, dtype):
    return jax.ShapeDtypeStruct(dims, dtype)


def lanes(ref, block, wide):
    return ref[:, pl.ds(pl.multiple_of(block * wide, wide), wide)]


def pair_at(place, dyh, dx):
    return (place[0] ^ dyh) * 4 + ((place[1] + dx) & 3)


def att_weights_kernel(place, *refs):
    blocks, wholes, sems = refs[:8], refs[8:10], refs[10]
    cols = blocks[0].shape[2]
    copies = []
    for other in (0, 1):
        half = place[2] ^ other
        for j in range(4):
            for i in range(4):
                dx = jnp.where(half == 0, i, j)
                e = jnp.where(half == 0, j, i)
                col = pl.ds(pl.multiple_of(((e & 1) * 2 + half) * cols, cols), cols)
                start = 0
                for whole in wholes:
                    rows = whole.shape[0] // 8
                    row = pl.ds(pl.multiple_of(pair_at(place, e >> 1, dx) * rows, rows), rows)
                    src = blocks[4 * other + j].at[i, pl.ds(start, rows)]
                    copies.append(pltpu.make_async_copy(src, whole.at[row, col], sems.at[len(copies)]))
                    start += rows
    for copy in copies:
        copy.start()
    for copy in copies:
        copy.wait()


def att_weights(place, blocks):
    rows, cols = blocks[0].shape[1:]
    return pl.pallas_call(
        att_weights_kernel,
        in_specs=[SMEM_SPEC] + [ANY_SPEC] * 8,
        out_specs=[VMEM_SPEC] * 2,
        out_shape=[shape((8 * (rows // 3 * k), 4 * cols), BF) for k in (2, 1)],
        scratch_shapes=[pltpu.SemaphoreType.DMA((64,))],
        compiler_params=BIG,
        cost_estimate=cost(7),
    )(place, *blocks)


def place_rows_kernel(first, *refs):
    lay_rows(first[0], refs[:-1], refs[-1])


def place_rows(pieces, first):
    rows, cols = pieces[0].shape
    return pl.pallas_call(
        place_rows_kernel,
        in_specs=[SMEM_SPEC] + [VMEM_SPEC] * 4,
        out_specs=VMEM_SPEC,
        out_shape=shape((4 * rows, cols), pieces[0].dtype),
        compiler_params=BIG,
        cost_estimate=cost(2),
    )(first, *pieces)


def project_kernel(first, p0, p1, p2, p3, gain, cos_ref, sine_ref, nq, kv, latent_own, whole):
    cols = p0.shape[1]
    for k, piece in enumerate((p0, p1, p2, p3)):
        at = ((first[0] + k) & 3) * cols
        whole[:, pl.ds(pl.multiple_of(at, cols), cols)] = piece[...]
    latent = whole[:, :QLAT].astype(F32)
    nq[...] = (latent * rms_scale(latent) * gain[...]).astype(BF)
    keys = whole[:, QLAT : QLAT + HDIM].astype(F32)
    kv[:, :HDIM] = turn(keys, cos_ref[...], sine_ref[...]).astype(BF)
    kv[:, HDIM:] = whole[:, QLAT + HDIM :]
    rows = latent_own.shape[0]
    latent_own[...] = whole[pl.ds(pl.multiple_of(first[0] * rows, rows), rows), :QLAT]


def project(first, pieces, gain, cos_table, sine_table):
    line, cols = pieces[0].shape
    return pl.pallas_call(
        project_kernel,
        in_specs=[SMEM_SPEC] + [VMEM_SPEC] * 7,
        out_specs=[VMEM_SPEC] * 3,
        out_shape=[shape((line, QLAT), BF), shape((line, 2 * HDIM), BF), shape((line // 4, QLAT), BF)],
        scratch_shapes=[pltpu.VMEM((line, 4 * cols), BF)],
        compiler_params=BIG,
        cost_estimate=cost(3.5),
    )(first, *pieces, gain, cos_table, sine_table)


def hidden_kernel(
    place, p0, p1, p2, p3, back, blocks, n2, o0, o1, o2, o3, hidden, turned, down, grads, weights, sems, out_sems
):
    half_cols, wide = blocks.shape[2] // 2, blocks.shape[3]
    count = weights.shape[1]
    copies = [[], []]
    for half in (0, 1):
        for slot in (0, 1):
            for d in range(blocks.shape[0] // 2):
                src = blocks.at[2 * d + (place[3] ^ slot), :, pl.ds(half * half_cols, half_cols)]
                row = (2 * half + slot) * half_cols
                dst = weights.at[:, pl.ds(row, half_cols), pl.ds(d * wide, wide)]
                at = half * 32 + len(copies[half])
                copies[half].append(pltpu.make_async_copy(src, dst, sems.at[at]))
    for copy in copies[0] + copies[1]:
        copy.start()
    outs = []
    for half in (0, 1):
        rows = pl.ds(half * 2 * half_cols, 2 * half_cols)
        outs.append(pltpu.make_async_copy(weights.at[2, rows], down.at[rows], out_sems.at[half]))
    lay_rows(None, (p0, p1, p2, p3), n2)

    def ready(half):
        for copy in copies[half]:
            copy.wait()
        outs[half].start()

    ready(0)
    for start in range(0, count, 256):
        size = min(256, count - start)
        if start <= 2 * half_cols < start + size:
            ready(1)
        rows = pl.ds(start, size)
        gate = mm_nt(n2[...], weights[0, rows])
        up = mm_nt(n2[...], weights[1, rows])
        grad = mm_nt(back[...], weights[2, rows])
        s = jax.nn.sigmoid(gate)
        silu = gate * s
        parts = [
            (grad * up * s * (1.0 + gate * (1.0 - s))).astype(BF),
            (grad * silu).astype(BF),
            (silu * up).astype(BF),
        ]
        grads[:, rows] = parts[0]
        grads[:, pl.ds(count + start, size)] = parts[1]
        quarter = hidden.shape[0] // 4
        for k in range(4):
            at = ((place[4] + k) & 3) * quarter
            hidden[pl.ds(pl.multiple_of(at, quarter), quarter), rows] = parts[2][k * quarter : (k + 1) * quarter]
        for m, tile in enumerate(parts):
            turned[m, rows] = tile.T
    rows = o0.shape[0]
    for start in range(0, n2.shape[1], 256):
        cols = pl.ds(start, 256)
        got = mm(grads[:, :count], weights[0, :, cols]) + mm(grads[:, count:], weights[1, :, cols])
        for k, part in enumerate((o0, o1, o2, o3)):
            part[:, cols] = got[k * rows : (k + 1) * rows].astype(BF)
    for copy in outs:
        copy.wait()


def hidden_units(place, n2_pieces, back_rows, blocks):
    line = back_rows.shape[0]
    cols, wide = blocks.shape[2:]
    whole = blocks.shape[0] // 2 * wide
    return pl.pallas_call(
        hidden_kernel,
        in_specs=[SMEM_SPEC] + [VMEM_SPEC] * 5 + [ANY_SPEC],
        out_specs=[VMEM_SPEC] * 7 + [ANY_SPEC],
        out_shape=[shape((line, whole), BF)]
        + [shape((line // 4, whole), BF)] * 4
        + [
            shape((line, 2 * cols), BF),
            shape((3, 2 * cols, line), BF),
            shape((2 * cols, whole), BF),
        ],
        scratch_shapes=[
            pltpu.VMEM((line, 4 * cols), BF),
            pltpu.VMEM((3, 2 * cols, whole), BF),
            pltpu.SemaphoreType.DMA((64,)),
            pltpu.SemaphoreType.DMA((2,)),
        ],
        compiler_params=BIG,
        cost_estimate=cost(22),
    )(place, *n2_pieces, back_rows, blocks)


def spot(place, slot, step):
    e = 2 * (step >> 2) + slot
    dx = step & 3
    first = place[2] == 0
    return jnp.where(first, e, dx), jnp.where(first, dx, e)


def hidden_grads_kernel(place, own, other, n2_own, n2_other, back_own, back_other, *refs):
    outs, buf, sems = refs[:4], refs[4], refs[5]
    mat, step = pl.program_id(0), pl.program_id(1)
    at = mat * pl.num_programs(1) + step
    turn_of = lax.rem(at, 2)
    rows, wide = outs[0].shape[3:]
    pair = pair_at(place, step >> 2, step & 3)

    def copy_to(turn, slot, i, j):
        return pltpu.make_async_copy(buf.at[turn, slot], outs[i].at[j, :, mat], sems.at[turn, slot])

    @pl.when(at >= 2)
    def _():
        for slot in (0, 1):
            copy_to(turn_of, slot, 0, 0).wait()

    def put(rows_own, rows_other):
        terms = mm(own[0], lanes(rows_own, pair, 2 * wide)) + mm(other[0], lanes(rows_other, pair, 2 * wide))
        terms = terms.astype(BF)
        for slot in (0, 1):
            for k in (0, 1):
                buf[turn_of, slot, k] = terms[slot * rows : (slot + 1) * rows, k * wide : (k + 1) * wide]

    @pl.when(mat < 2)
    def _():
        put(n2_own, n2_other)

    @pl.when(mat == 2)
    def _():
        put(back_own, back_other)

    for slot in (0, 1):
        i, j = spot(place, slot, step)
        for n in range(4):

            @pl.when(i == n)
            def _():
                copy_to(turn_of, slot, n, j).start()

    @pl.when(at == pl.num_programs(0) * pl.num_programs(1) - 1)
    def _():
        for turn in (0, 1):
            for slot in (0, 1):
                copy_to(turn, slot, 0, 0).wait()


def hidden_grads(place, own, other, n2_own, n2_other, back_own, back_other):
    count, line = own.shape[1:]
    cols = count // 2
    wide = n2_own.shape[1] // 16
    units_spec = pl.BlockSpec((1, cols, line), lambda m, t, place: (m, place[2], 0))
    rows_spec = pl.BlockSpec(n2_own.shape, lambda m, t, place: (0, 0))
    return pl.pallas_call(
        hidden_grads_kernel,
        grid_spec=pltpu.PrefetchScalarGridSpec(
            num_scalar_prefetch=1,
            grid=(3, 8),
            in_specs=[units_spec] * 2 + [rows_spec] * 4,
            out_specs=[ANY_SPEC] * 4,
            scratch_shapes=[
                pltpu.VMEM((2, 2, 2, cols // 2, wide), BF),
                pltpu.SemaphoreType.DMA((2, 2)),
            ],
        ),
        out_shape=[shape((4, 2, 3, cols // 2, wide), BF)] * 4,
        compiler_params=BIG,
        cost_estimate=cost(23),
    )(place, own, other, n2_own, n2_other, back_own, back_other)


def att_grads_kernel(place, dh_own, dh_other, nq_own, nq_other, a_own, a_other, g_own, g_other, dst):
    rows = dh_own.shape[1]
    wide = dst.shape[4]
    both = lambda a, b: jnp.concatenate([a[...], b[...]], axis=0)
    out_terms = mm_tn(both(dh_own, dh_other), both(a_own, a_other)).astype(BF)
    query_terms = mm_tn(both(nq_own, nq_other), both(g_own, g_other)).astype(BF)
    for h in range(dst.shape[2]):
        cols = slice(h * wide, (h + 1) * wide)
        dst[0, 0, h, :rows] = out_terms[:, cols]
        dst[0, 0, h, rows:] = query_terms[:, cols]


def att_grads(place, dh, nq, attended, grad_pre):
    line = dh[0].shape[0]
    out_rows, query_rows = dh[0].shape[1] // 8, nq[0].shape[1] // 8
    cols = attended[0].shape[1] // 4
    pair = lambda wide: pl.BlockSpec((line, wide), lambda s, t, place: (0, pair_at(place, t >> 2, t & 3)))
    half = pl.BlockSpec((line, cols), lambda s, t, place: (0, 2 * s + place[2]))
    return pl.pallas_call(
        att_grads_kernel,
        grid_spec=pltpu.PrefetchScalarGridSpec(
            num_scalar_prefetch=1,
            grid=(2, 8),
            in_specs=[pair(out_rows)] * 2 + [pair(query_rows)] * 2 + [half] * 4,
            out_specs=pl.BlockSpec(
                (1, 1, 2, out_rows + query_rows, cols // 2),
                lambda s, t, place: spot(place, s, t) + (0, 0, 0),
            ),
        ),
        out_shape=shape((4, 4, 2, out_rows + query_rows, cols // 2), BF),
        compiler_params=BIG,
        cost_estimate=cost(15),
    )(place, *dh, *nq, *attended, *grad_pre)


def lay_rows(first, pieces, out):
    rows = pieces[0].shape[0]
    for k, piece in enumerate(pieces):
        if first is None:
            out[k * rows : (k + 1) * rows] = piece[...]
        else:
            at = ((first + k) & 3) * rows
            out[pl.ds(pl.multiple_of(at, rows), rows)] = piece[...]


def entry_kernel(place, first, p0, p1, p2, p3, own, other, out, rows):
    lay_rows(first[0], (p0, p1, p2, p3), rows)
    total = 0.0
    wide = own.shape[2]
    for dc, buf in enumerate((own, other)):
        for dx in range(4):
            left = [
                lanes(rows, pair_at(place, dyh, dx) * 2 + (place[2] ^ dc), wide) for dyh in (0, 1)
            ]
            total = total + mm(jnp.concatenate(left, axis=1), buf[dx].reshape(2 * wide, -1))
    out[...] = total.astype(BF)


def entry_project(place, first, pieces, own, other):
    rows, width = pieces[0].shape
    return pl.pallas_call(
        entry_kernel,
        in_specs=[SMEM_SPEC] * 2 + [VMEM_SPEC] * 6,
        out_specs=[VMEM_SPEC] * 2,
        out_shape=[shape((4 * rows, own.shape[3]), BF), shape((4 * rows, width), BF)],
        compiler_params=BIG,
        cost_estimate=cost(5),
    )(place, first, *pieces, own, other)


def entry_grads_kernel(place, n1_own, n1_other, df_own, df_other, dst):
    wide = dst.shape[2]
    right = jnp.concatenate([df_own[...], df_other[...]], axis=0)
    for dyh in (0, 1):
        for dx in range(4):
            block = pair_at(place, dyh, dx) * 2 + place[2]
            left = jnp.concatenate([lanes(n1_own, block, wide), lanes(n1_other, block, wide)], axis=0)
            dst[dyh, dx] = mm_tn(left, right).astype(BF)


def entry_grads(place, n1_own, n1_other, df_own, df_other):
    return pl.pallas_call(
        entry_grads_kernel,
        in_specs=[SMEM_SPEC] + [VMEM_SPEC] * 4,
        out_specs=VMEM_SPEC,
        out_shape=shape((2, 4, n1_own.shape[1] // 16, df_own.shape[1]), BF),
        compiler_params=BIG,
        cost_estimate=cost(4.5),
    )(place, n1_own, n1_other, df_own, df_other)


def finish_kernel(grad_first, whole, x_ref, mid_ref, gain_ref, grad_out, gain_row):
    grad = mm_nt(grad_first[...], whole[...])
    x = x_ref[...].astype(F32)
    scale = rms_scale(x)
    unit = x * scale
    gain_row[...] = jnp.sum(grad * unit, axis=0, keepdims=True)
    grad_out[...] = mid_ref[...] + norm_back(grad, unit, scale, gain_ref[...])


def finish(grad_first, whole, tokens, grad_middle, gain_one):
    rows = tokens.shape[0]
    return pl.pallas_call(
        finish_kernel,
        in_specs=[VMEM_SPEC] * 5,
        out_specs=[VMEM_SPEC] * 2,
        out_shape=[shape((rows, D), F32), shape((1, D), F32)],
        compiler_params=BIG,
        cost_estimate=cost(6.5),
    )(grad_first, whole, tokens, grad_middle, gain_one)


def turn(values, cos_table, sine_table):
    half = values.shape[1] // 2
    left, right = values[:, :half], values[:, half:]
    return jnp.concatenate(
        [left * cos_table - right * sine_table, left * sine_table + right * cos_table], axis=1
    )


def give_rows(first, source, pieces):
    rows = pieces[0].shape[0]
    for k, piece in enumerate(pieces):
        at = ((first + k) & 3) * rows
        piece[...] = source[pl.ds(pl.multiple_of(at, rows), rows)].astype(piece.dtype)


def attend_kernel(
    info, nq, query_w, kv_own, kv_other, starts, cos_ref, sine_ref, out_w,
    q_out, out, w_own, w_other, o0, o1, o2, o3, branch,
):
    yl = info[0]
    head = pl.program_id(0)
    line = nq.shape[0]
    block = 128
    queries = turn(mm(nq[...], query_w[...]), cos_ref[...], sine_ref[...]).astype(BF)
    q_out[...] = queries
    scale = HDIM ** (-0.5)

    def work(with_other):
        for at in range(0, line, block):
            end = at + block
            q = queries[at:end]
            first = starts[at:end] - yl * line
            own = mm_nt(q, kv_own[:end, :HDIM]) * scale
            spot = lax.broadcasted_iota(jnp.int32, (block, end), 1)
            row = at + lax.broadcasted_iota(jnp.int32, (block, end), 0)
            own = jnp.where((spot <= row) & (spot >= first), own, MASKED)
            top = jnp.max(own, axis=1, keepdims=True)
            if with_other:
                far = mm_nt(q, kv_other[:, :HDIM]) * scale
                far_spot = lax.broadcasted_iota(jnp.int32, (block, line), 1) - line
                far = jnp.where(far_spot >= first, far, MASKED)
                top = jnp.maximum(top, jnp.max(far, axis=1, keepdims=True))
                far = jnp.exp(far - top)
            own = jnp.exp(own - top)
            total = jnp.sum(own, axis=1, keepdims=True)
            if with_other:
                total = total + jnp.sum(far, axis=1, keepdims=True)
            share = 1.0 / total
            own = (own * share).astype(BF)
            w_own[0, at:end, :end] = own
            if end < line:
                w_own[0, at:end, end:] = jnp.zeros((block, line - end), BF)
            result = mm(own, kv_own[:end, HDIM:])
            if with_other:
                far = (far * share).astype(BF)
                w_other[0, at:end] = far
                result = result + mm(far, kv_other[:, HDIM:])
            out[at:end] = result.astype(BF)

    @pl.when(yl == 0)
    def _():
        work(False)

    @pl.when(yl == 1)
    def _():
        work(True)

    part = mm_nt(out[...], out_w[...])

    @pl.when(head == 0)
    def _():
        branch[...] = part

    @pl.when(head > 0)
    def _():
        branch[...] += part

    @pl.when(head == pl.num_programs(0) - 1)
    def _():
        give_rows(info[1], branch, (o0, o1, o2, o3))


def attend(info, nq, query_low, kv_own, kv_other, starts, cos_table, sine_table, out_low):
    line = nq.shape[0]
    width = query_low.shape[1]
    heads = width // HDIM
    whole = lambda v: pl.BlockSpec(v.shape, lambda h: (0, 0))
    head = pl.BlockSpec((line, HDIM), lambda h: (0, h))
    weight = lambda v: pl.BlockSpec((v.shape[0], HDIM), lambda h: (0, h))
    weights = pl.BlockSpec((1, line, line), lambda h: (h, 0, 0))
    piece = (line // 4, out_low.shape[0])
    return pl.pallas_call(
        attend_kernel,
        grid=(heads,),
        in_specs=[SMEM_SPEC, whole(nq), weight(query_low)]
        + [whole(v) for v in (kv_own, kv_other, starts, cos_table, sine_table)]
        + [weight(out_low)],
        out_specs=[head, head, weights, weights] + [pl.BlockSpec(piece, lambda h: (0, 0))] * 4,
        out_shape=[shape((line, width), BF)] * 2
        + [shape((heads, line, line), BF)] * 2
        + [shape(piece, BF)] * 4,
        scratch_shapes=[pltpu.VMEM((line, out_low.shape[0]), F32)],
        compiler_params=BIG,
        cost_estimate=cost(16),
    )(info, nq, query_low, kv_own, kv_other, starts, cos_table, sine_table, out_low)


def attend_back_kernel(
    info, p0, p1, p2, p3, out_w, out, queries, kv_own, kv_other, w_own, w_other, cos_ref, sine_ref, query_w,
    dh, grad_q, o0, o1, o2, o3, scores, k_own, v_own, k_far, v_far, grad_nq, sums,
):
    yl = info[0]
    head = pl.program_id(0)
    line = queries.shape[0]
    block = 128
    scale = HDIM ** (-0.5)

    @pl.when(head == 0)
    def _():
        lay_rows(info[1], (p0, p1, p2, p3), dh)
        for ref in (k_own, v_own, k_far, v_far, grad_nq):
            ref[...] = jnp.zeros_like(ref)

    g = mm(dh[...], out_w[...]).astype(BF)
    delta = jnp.sum(g.astype(F32) * out[...].astype(F32), axis=1, keepdims=True)

    def work(with_other):
        for at in range(0, line, block):
            end = at + block
            own = mm_nt(g[at:end], kv_own[:end, HDIM:]) - delta[at:end]
            own = (w_own[0, at:end, :end].astype(F32) * own).astype(BF)
            scores[at:end, :end] = own
            grad = mm(own, kv_own[:end, :HDIM])
            if with_other:
                far = mm_nt(g[at:end], kv_other[:, HDIM:]) - delta[at:end]
                far = (w_other[0, at:end].astype(F32) * far).astype(BF)
                scores[at:end, line:] = far
                grad = grad + mm(far, kv_other[:, :HDIM])
            grad_q[at:end] = turn(grad * scale, cos_ref[at:end], -sine_ref[at:end]).astype(BF)
        for at in range(0, line, block):
            end = at + block
            k_own[at:end] += mm_tn(scores[at:, at:end], queries[at:])
            v_own[at:end] += mm_tn(w_own[0, at:, at:end], g[at:])
        if with_other:
            k_far[...] += mm_tn(scores[:, line:], queries[...])
            v_far[...] += mm_tn(w_other[0], g)

    @pl.when(yl == 0)
    def _():
        work(False)

    @pl.when(yl == 1)
    def _():
        work(True)

    grad_nq[...] += mm_nt(grad_q[...], query_w[...])

    @pl.when(head == pl.num_programs(0) - 1)
    def _():
        width = grad_nq.shape[1]
        sums[:, :width] = grad_nq[...]
        for i, (ref, factor) in enumerate(((k_own, scale), (v_own, 1.0), (k_far, scale), (v_far, 1.0))):
            sums[:, width + i * HDIM : width + (i + 1) * HDIM] = ref[...] * factor
        give_rows(info[1], sums, (o0, o1, o2, o3))


def attend_back(
    info, dh_pieces, out_low, out, queries, kv_own, kv_other, w_own, w_other, cos_table, sine_table, query_low
):
    line, width = queries.shape
    heads = width // HDIM
    latent = query_low.shape[0]
    whole = lambda v: pl.BlockSpec(v.shape, lambda h: (0, 0))
    head = pl.BlockSpec((line, HDIM), lambda h: (0, h))
    weight = lambda v: pl.BlockSpec((v.shape[0], HDIM), lambda h: (0, h))
    weights = pl.BlockSpec((1, line, line), lambda h: (h, 0, 0))
    piece = (line // 4, latent + 4 * HDIM)
    rows = (line, out_low.shape[0])
    return pl.pallas_call(
        attend_back_kernel,
        grid=(heads,),
        in_specs=[SMEM_SPEC]
        + [whole(v) for v in dh_pieces]
        + [weight(out_low), head, head, whole(kv_own), whole(kv_other), weights, weights]
        + [whole(cos_table), whole(sine_table), weight(query_low)],
        out_specs=[pl.BlockSpec(rows, lambda h: (0, 0)), head] + [pl.BlockSpec(piece, lambda h: (0, 0))] * 4,
        out_shape=[shape(rows, BF), shape((line, width), BF)] + [shape(piece, BF)] * 4,
        scratch_shapes=[pltpu.VMEM((line, 2 * line), BF)]
        + [pltpu.VMEM((line, HDIM), F32)] * 4
        + [pltpu.VMEM((line, latent), F32), pltpu.VMEM((line, piece[1]), F32)],
        compiler_params=BIG,
        cost_estimate=cost(16),
    )(
        info, *dh_pieces, out_low, out, queries, kv_own, kv_other, w_own, w_other, cos_table, sine_table, query_low
    )


def local(
    tokens,
    cotangent,
    doc_lengths,
    entry_weight,
    entry_first,
    entry_second,
    entry_average,
    query_weight,
    query_first,
    query_second,
    query_average,
    out_weight,
    out_first,
    out_second,
    out_average,
    ffn_weight,
    ffn_first,
    ffn_second,
    ffn_average,
    norm_gains,
    gains_first,
    gains_second,
    gains_average,
):
    rows = tokens.shape[0]
    line = 4 * rows
    z, yl, c = lax.axis_index("z"), lax.axis_index("yl"), lax.axis_index("c")
    place = jnp.stack([lax.axis_index(a) for a in ("yh", "x", "c", "yl", "z")]).astype(jnp.int32)
    wide = D // 16
    ffn_cols = ffn_weight.shape[2]
    half_cols = ffn_cols // 2
    entry_cols = entry_weight.shape[1]
    slot_cols = entry_cols // 4
    head_cols = query_weight.shape[1]
    gain_one = 1.0 + norm_gains[None, :D]
    gain_query = 1.0 + norm_gains[D : D + QLAT]
    gain_two = 1.0 + norm_gains[None, D + QLAT :]

    ffn_low = jnp.transpose(ffn_weight, (1, 2, 0)).astype(BF)

    inputs = tokens.astype(F32)
    scale_one = rms_scale(inputs)
    normed_one = (inputs * scale_one * gain_one).astype(BF)
    first = z[None].astype(jnp.int32)
    start = jnp.zeros((1,), jnp.int32)
    n1_near = ring_near(normed_one)

    entry_low = entry_weight.astype(BF)
    slot = lax.dynamic_slice_in_dim(entry_low, z * slot_cols, slot_cols, 1)
    slot = jnp.stack([slot, from_y(slot, 3)])
    slot = jnp.stack([slot] + [from_x(slot, k) for k in (1, 2, 3)])
    n1_pieces = ring_pieces(normed_one, n1_near)
    slot, *n1_pieces = tie(slot, *n1_pieces)
    slot_other = from_c(slot)

    att_half = head_cols // 2
    halves = [
        (out_weight[:, h * att_half : (h + 1) * att_half], query_weight[:, h * att_half : (h + 1) * att_half])
        for h in (0, 1)
    ]
    keep, give = by_core(*[jnp.concatenate(h, axis=0).astype(BF) for h in halves])
    got = from_c(give)
    att_0, att_1 = by_core(keep, got)
    att_own = jnp.concatenate([att_0[:wide], att_1[:wide], att_0[wide:], att_1[wide:]], axis=0)
    att_near = gather_near(att_own)

    f_slot, n1_rows = entry_project(place, first, n1_pieces, slot, slot_other)
    f_slot, doc_lengths, att_near = tie(f_slot, doc_lengths, att_near)
    *tied, ffn_low = tie(*gather_far(att_near), *ring_pieces(f_slot), ffn_low)
    att_far, f_pieces = tied[:4], tied[4:]
    ffn_all = lax.all_gather(ffn_low, PLANE, axis=0, tiled=False)
    places_all, segment_all, offset_all = doc_layout(doc_lengths[0], 2 * line)
    line_offset = lax.dynamic_slice_in_dim(offset_all, yl * line, line)
    line_places = yl * line + jnp.arange(line, dtype=jnp.int32)
    starts = (line_places - line_offset)[:, None]
    cos_line, sine_line = rope_tables(line_offset, HDIM // 2)
    query_rows, kv_own, latent_own = project(
        first, f_pieces, gain_query[None], cos_line, sine_line
    )
    kv_other = from_y(kv_own, 1)
    info = place[3:]
    kv_other, *att_far = tie(kv_other, *att_far)
    out_low, query_low = att_weights(place, att_far + [from_c(v) for v in att_far])
    out_low, cot_late = tie(out_low, cotangent)
    back_pieces = line_pieces(cot_late)
    queries, attended, w_own, w_other, *branch = attend(
        info, query_rows, query_low, kv_own, kv_other, starts, cos_line, sine_line, out_low
    )

    *tied, back_pieces[0] = tie(*branch, *back_pieces[1:], back_pieces[0])
    branch, back_pieces[1:] = tied[:4], tied[4:]
    *branch, back_rows = tie(*line_sum(*branch), place_rows(back_pieces, start))
    middle = inputs + total(branch)
    scale_two = rms_scale(middle)
    unit_two = middle * scale_two
    normed_two = (unit_two * gain_two).astype(BF)

    n2_pieces = ring_pieces(normed_two)
    back_other, query_other, attended_other = from_c(back_rows), from_c(query_rows), from_c(attended)
    back_other, query_other, attended_other, entry_low, ffn_all, *n2_pieces = tie(
        back_other, query_other, attended_other, entry_low, ffn_all, *n2_pieces
    )
    entry_all = lax.all_gather(entry_low, DP, axis=0, tiled=True)
    n2_rows, *n2_parts, hidden_low, turned, down_low = hidden_units(place, n2_pieces, back_rows, ffn_all)
    ffn_terms = hidden_grads(
        place, turned, from_c(turned), n2_rows, from_c(n2_rows), back_rows, back_other
    )
    tied = tie(*line_sum(*n2_parts), *ffn_terms)
    grad_normed_two, ffn_terms = total(tied[:4]), tied[4:]
    ffn_far = far_moves(ffn_terms)
    grad_middle = cotangent.astype(F32) + norm_back(grad_normed_two, unit_two, scale_two, gain_two)
    dh_pieces = line_pieces(grad_middle.astype(BF))
    mixed_part = mm(hidden_low, down_low).astype(BF)
    *dh_pieces, mixed_part, entry_all = tie(*dh_pieces, mixed_part, entry_all)
    mixed = lax.psum_scatter(mixed_part, "z", scatter_dimension=0, tiled=True)
    mixed_out = (middle + mixed.astype(F32)).astype(BF)

    dh_rows, grad_query_pre, *sums = attend_back(
        info, dh_pieces, out_low, attended, queries, kv_own, kv_other, w_own, w_other,
        cos_line, sine_line, query_low,
    )
    *sums, ffn_far[1], ffn_far[2] = tie(*sums, ffn_far[1], ffn_far[2])
    summed = line_sum(*sums)
    pair = lambda v: (v, from_c(v))
    att_terms = att_grads(
        place, pair(dh_rows), (query_rows, query_other), (attended, attended_other), pair(grad_query_pre)
    )
    *summed, att_terms = tie(*summed, att_terms)
    summed = total(summed)
    grad_normed_query = summed[:, :QLAT]
    kv_got = from_y(summed[:, QLAT + 2 * HDIM :].astype(BF), 1)
    kv_got, ffn_far[3] = tie(kv_got, ffn_far[3])
    att_far = far_moves(att_terms)
    kv_grad = summed[:, QLAT : QLAT + 2 * HDIM] + kv_got.astype(F32)
    own = lambda v: rows_of(v, 0, rows)
    latent = latent_own.astype(F32)
    scale_query = rms_scale(latent)
    unit_query = latent * scale_query
    grad_latent = norm_back(grad_normed_query, unit_query, scale_query, gain_query)
    grad_first = jnp.concatenate(
        [grad_latent, rotate(kv_grad[:, :HDIM], own(cos_line), -own(sine_line)), kv_grad[:, HDIM:]], axis=1
    ).astype(BF)

    input_grad, one_row = finish(grad_first, entry_all, tokens, grad_middle, gain_one)

    low = jnp.concatenate([total(v).astype(BF).reshape(4, -1, wide) for v in (ffn_far, att_far)], axis=1)
    got = sum_near(low)
    ffn_rows = 6 * half_cols
    ffn_got = got[:ffn_rows].reshape(2, -1, wide)
    att_got = got[ffn_rows:].reshape(2, 3 * wide, wide)
    for_core = [
        jnp.concatenate(
            [ffn_got[n]]
            + [
                att_got[h, a * wide + n * b : a * wide + (n + 1) * b]
                for h in (0, 1)
                for a, b in ((0, wide), (2, wide // 2))
            ],
            axis=0,
        )
        for n in (0, 1)
    ]
    mine, theirs = by_core(*for_core)
    halves = by_core(mine, from_c(theirs.astype(BF)).astype(F32))
    ffn_rows = ffn_rows // 2
    ffn_grad = jnp.concatenate([v[:ffn_rows].reshape(3, half_cols, wide) for v in halves], axis=1)
    ffn_grad = jnp.transpose(ffn_grad, (2, 0, 1))
    att_grad = jnp.concatenate(
        [v[ffn_rows + h * 3 * wide // 2 :][: 3 * wide // 2] for v in halves for h in (0, 1)], axis=1
    )
    out_grad, query_grad = att_grad[:wide], att_grad[wide:]

    gain_terms = jnp.concatenate(
        [
            one_row[0],
            jnp.sum(grad_normed_query * unit_query, axis=0),
            jnp.sum(grad_normed_two * unit_two, axis=0),
        ]
    )
    gain_count = gain_terms.shape[0]
    gain_height = -(-gain_count // (16 * slot_cols)) * 16

    def with_gains(value, gains):
        padded = jnp.pad(gains, (0, gain_height * slot_cols - gain_count))
        return jnp.concatenate([value, padded.reshape(gain_height, slot_cols).astype(BF)], axis=0)

    def split_gains(message):
        got = message[-gain_height:].astype(F32).reshape(-1)[:gain_count]
        return message[:-gain_height], got

    def exchange(values, moves, gains):
        sent = [split_gains(step(with_gains(v, gains))) for v, step in zip(values, moves)]
        return [v for v, _ in sent], gains + sum(g for _, g in sent)

    cols_of = lambda k: lax.dynamic_slice_in_dim(grad_first, ((z + k) % 4) * slot_cols, slot_cols, 1)
    df_slot = place_rows([cols_of(0)] + [from_z(cols_of(4 - k), k) for k in (1, 2, 3)], first)
    (df_other,), gains_grad = exchange([df_slot], [from_c], gain_terms)
    entry_terms = entry_grads(place, n1_rows, from_c(n1_rows), df_slot, df_other)
    got, gains_grad = exchange(
        [entry_terms[:, k].reshape(2 * wide, slot_cols) for k in (1, 2, 3)],
        [lambda v, k=k: from_x(v, 4 - k) for k in (1, 2, 3)],
        gains_grad,
    )
    part = sum((v.astype(F32) for v in got), entry_terms[:, 0].reshape(2 * wide, slot_cols).astype(F32))
    low = part.astype(BF).reshape(2, wide, slot_cols)
    got, gains_grad = exchange(
        [low[e >> 1] for e in (1, 2, 3)], [lambda v, e=e: from_y(v, e) for e in (1, 2, 3)], gains_grad
    )
    low = sum((v.astype(F32) for v in got), part[:wide]).astype(BF)
    got, gains_grad = exchange(
        [low] * 3, [lambda v, k=k: from_z(v, k) for k in (1, 2, 3)], gains_grad
    )
    entry_grad = jnp.zeros((wide, entry_cols), BF)
    for k, piece in enumerate([low] + got):
        entry_grad = lax.dynamic_update_slice_in_dim(entry_grad, piece, ((z + k) % 4) * slot_cols, 1)
    entry_grad = entry_grad.astype(F32)

    return (
        (mixed_out, input_grad)
        + full_step(entry_weight, entry_first, entry_second, entry_average, entry_grad, ENTRY_RATE, DECAY)
        + full_step(query_weight, query_first, query_second, query_average, query_grad, QUERY_RATE, DECAY)
        + full_step(out_weight, out_first, out_second, out_average, out_grad, OUT_RATE, DECAY)
        + full_step(ffn_weight, ffn_first, ffn_second, ffn_average, ffn_grad, FFN_RATE, DECAY)
        + full_step(norm_gains, gains_first, gains_second, gains_average, gains_grad, GAIN_RATE, 0.0)
    )


def solution(mesh):
    fine = Mesh(mesh.devices.reshape(tuple(SIZES[a] for a in AXES)), AXES)
    tokens = P(AXES, None)
    entry = P(DP, None)
    middle = P(DP, SEQ)
    ffn = P(DP, None, SEQ)
    gains = P()
    return jax.shard_map(
        local,
        mesh=fine,
        in_specs=(tokens, tokens, entry) + (entry,) * 4 + (middle,) * 8 + (ffn,) * 4 + (gains,) * 4,
        out_specs=(tokens, tokens) + (entry,) * 5 + (middle,) * 10 + (ffn,) * 5 + (gains,) * 5,
        check_vma=False,
    )
```

```python
import functools

import jax
import jax.numpy as jnp
import numpy as np
from jax import lax
from jax.experimental import pallas as pl
from jax.experimental.pallas import tpu as pltpu
from jax.sharding import Mesh, PartitionSpec as P

D = 2048
QLAT = 1024
HDIM = 256
STEP = 10
EPS = 1e-05
THETA = 10000.0
BETA_ONE = 0.9
BETA_TWO = 0.95
ADAM_EPS = 1e-08
ENTRY_RATE = 0.03
QUERY_RATE = 0.04
OUT_RATE = 0.08
FFN_RATE = 0.03
GAIN_RATE = 0.1
DECAY = 0.1
MASKED = -1e30
SIZES = {"yh": 2, "x": 4, "c": 2, "yl": 2, "z": 4}
AXES = ("yh", "x", "c", "yl", "z")
BF = jnp.bfloat16
F32 = jnp.float32


def move(value, axes, source):
    dims = [SIZES[a] for a in axes]
    pairs = []
    for place in np.ndindex(*dims):
        src = source(dict(zip(axes, place)))
        src_place = [src[a] % SIZES[a] for a in axes]
        pairs.append((int(np.ravel_multi_index(src_place, dims)), int(np.ravel_multi_index(place, dims))))
    return lax.ppermute(value, axes, pairs)


def from_z(value, k):
    return move(value, ("z",), lambda d: {"z": d["z"] + k})


def from_x(value, k):
    return move(value, ("x",), lambda d: {"x": d["x"] + k})


def from_y(value, e):
    return move(value, ("yh", "yl"), lambda d: {"yh": d["yh"] ^ (e >> 1), "yl": d["yl"] ^ (e & 1)})


def from_c(value):
    return move(value, ("c",), lambda d: {"c": d["c"] ^ 1})


def line_pieces(value):
    return [value] + [from_z(value, k) for k in (1, 2, 3)]


def ring_near(value):
    return from_z(value, 1), from_z(value, 3)


def ring_pieces(value, near=None):
    half = value.shape[0] // 2
    after, before = near or ring_near(value)
    top = from_z(after[:half], 1)
    bottom = from_z(before[half:], 3)
    return [value, after, jnp.concatenate([top, bottom], axis=0), before]


def add_low(left, right):
    return (left.astype(F32) + right.astype(F32)).astype(BF)


def total(values):
    return sum((v.astype(F32) for v in values[1:]), values[0].astype(F32))


def line_sum(p0, p1, p2, p3):
    return [p0, from_z(p2, 2), from_z(p1, 3), from_z(p3, 1)]


def ring_sum(p0, p1, p2, p3):
    half = p2.shape[0] // 2
    got_top = from_z(p2[:half], 3)
    got_bottom = from_z(p2[half:], 1)
    p1 = jnp.concatenate([add_low(p1[:half], got_top), p1[half:]], axis=0)
    p3 = jnp.concatenate([p3[:half], add_low(p3[half:], got_bottom)], axis=0)
    return [p0, from_z(p1, 3), from_z(p3, 1)]


def rows_of(whole, k, rows):
    z = lax.axis_index("z")
    return lax.dynamic_slice_in_dim(whole, ((z + k) % 4) * rows, rows, 0)


def tie(*values):
    return lax.optimization_barrier(values)


PLANE = ("yh", "x", "c", "yl")
DP = ("yh", "x", "c")
SEQ = ("yl", "z")


def one_way(value, k, along_x, send):
    def source(d):
        if d["c"] in along_x:
            return dict(d, x=d["x"] + (4 - k if send else k))
        return dict(d, yh=d["yh"] ^ (k >> 1), yl=d["yl"] ^ (k & 1))

    return move(value, PLANE, source)


def gather_near(value):
    return jnp.stack([value] + [one_way(value, k, (0,), False) for k in (1, 2, 3)])


def gather_far(near):
    return [near] + [one_way(near, k, (1,), False) for k in (1, 2, 3)]


def far_moves(terms):
    return [terms[0]] + [one_way(terms[k], k, (1,), True) for k in (1, 3, 2)]


def sum_near(low):
    total = low[0].astype(F32)
    for k in (1, 2, 3):
        total = total + one_way(low[k], k, (0,), True).astype(F32)
    return total


def by_core(first, second):
    c = lax.axis_index("c")
    return jnp.where(c == 0, first, second), jnp.where(c == 0, second, first)


def doc_layout(lengths, token_count):
    ends = jnp.cumsum(lengths)
    starts = ends - lengths
    places = jnp.arange(token_count, dtype=jnp.int32)
    inside = (places[:, None] >= starts[None, :]) & (places[:, None] < ends[None, :])
    labels = jnp.arange(lengths.shape[0], dtype=jnp.int32)
    segment = jnp.sum(jnp.where(inside, labels[None, :], 0), axis=1)
    offset = places - jnp.sum(jnp.where(inside, starts[None, :], 0), axis=1)
    return (places, segment, offset)


def rope_tables(offset, half_dim):
    freqs = THETA ** (-jnp.arange(half_dim, dtype=F32) * 2.0 / (2.0 * half_dim))
    angles = offset.astype(F32)[:, None] * freqs[None, :]
    return (jnp.cos(angles), jnp.sin(angles))


def rotate(values, cos_table, sine_table):
    half_dim = values.shape[-1] // 2
    left_half = values[..., :half_dim]
    right_half = values[..., half_dim:]
    return jnp.concatenate(
        [
            left_half * cos_table - right_half * sine_table,
            left_half * sine_table + right_half * cos_table,
        ],
        axis=-1,
    )


def rms_scale(values):
    return lax.rsqrt(jnp.mean(values * values, axis=-1, keepdims=True) + EPS)


def norm_back(grad_normed, unit_rows, scale_rows, gain_row):
    scaled = grad_normed * gain_row
    return scale_rows * (scaled - unit_rows * jnp.mean(scaled * unit_rows, axis=-1, keepdims=True))


def adamw_step(weight, moment, squares, grad, rate, decay):
    moment_new = BETA_ONE * moment + (1.0 - BETA_ONE) * grad
    squares_new = BETA_TWO * squares + (1.0 - BETA_TWO) * grad * grad
    first_fix = 1.0 - BETA_ONE**STEP
    second_fix = 1.0 - BETA_TWO**STEP
    update = moment_new / first_fix / (jnp.sqrt(squares_new / second_fix) + ADAM_EPS)
    master = weight - rate * (update + decay * weight)
    return (moment_new, squares_new, master)


def full_step(weight, moment, squares, average, grad, rate, decay):
    keep = min(0.999, (1.0 + STEP) / (10.0 + STEP))
    moment_new, squares_new, master = adamw_step(weight, moment, squares, grad, rate, decay)
    return (grad, moment_new, squares_new, master, keep * average + (1.0 - keep) * master)


def mm(left, right):
    return jnp.dot(left, right, preferred_element_type=F32)


def mm_nt(left, right):
    return lax.dot_general(left, right, (((1,), (1,)), ((), ())), preferred_element_type=F32)


def mm_tn(left, right):
    return lax.dot_general(left, right, (((0,), (0,)), ((), ())), preferred_element_type=F32)


VMEM_SPEC = pl.BlockSpec(memory_space=pltpu.VMEM)
SMEM_SPEC = pl.BlockSpec(memory_space=pltpu.SMEM)
ANY_SPEC = pl.BlockSpec(memory_space=pl.ANY)
BIG = pltpu.CompilerParams(vmem_limit_bytes=56 * 1024 * 1024)


def cost(micros):
    return pl.CostEstimate(
        flops=int(micros * 1.1e9), bytes_accessed=int(micros * 3.3e6), transcendentals=0
    )


def shape(dims, dtype):
    return jax.ShapeDtypeStruct(dims, dtype)


def lanes(ref, block, wide):
    return ref[:, pl.ds(pl.multiple_of(block * wide, wide), wide)]


def pair_at(place, dyh, dx):
    return (place[0] ^ dyh) * 4 + ((place[1] + dx) & 3)


def att_weights_kernel(place, *refs):
    blocks, wholes, sems = refs[:8], refs[8:10], refs[10]
    cols = blocks[0].shape[2]
    copies = []
    for other in (0, 1):
        half = place[2] ^ other
        for j in range(4):
            for i in range(4):
                dx = jnp.where(half == 0, i, j)
                e = jnp.where(half == 0, j, i)
                col = pl.ds(pl.multiple_of(((e & 1) * 2 + half) * cols, cols), cols)
                start = 0
                for whole in wholes:
                    rows = whole.shape[0] // 8
                    row = pl.ds(pl.multiple_of(pair_at(place, e >> 1, dx) * rows, rows), rows)
                    src = blocks[4 * other + j].at[i, pl.ds(start, rows)]
                    copies.append(pltpu.make_async_copy(src, whole.at[row, col], sems.at[len(copies)]))
                    start += rows
    for copy in copies:
        copy.start()
    for copy in copies:
        copy.wait()


def att_weights(place, blocks):
    rows, cols = blocks[0].shape[1:]
    return pl.pallas_call(
        att_weights_kernel,
        in_specs=[SMEM_SPEC] + [ANY_SPEC] * 8,
        out_specs=[VMEM_SPEC] * 2,
        out_shape=[shape((8 * (rows // 3 * k), 4 * cols), BF) for k in (2, 1)],
        scratch_shapes=[pltpu.SemaphoreType.DMA((64,))],
        compiler_params=BIG,
        cost_estimate=cost(7),
    )(place, *blocks)


def place_rows_kernel(first, *refs):
    lay_rows(first[0], refs[:-1], refs[-1])


def place_rows(pieces, first):
    rows, cols = pieces[0].shape
    return pl.pallas_call(
        place_rows_kernel,
        in_specs=[SMEM_SPEC] + [VMEM_SPEC] * 4,
        out_specs=VMEM_SPEC,
        out_shape=shape((4 * rows, cols), pieces[0].dtype),
        compiler_params=BIG,
        cost_estimate=cost(2),
    )(first, *pieces)


def project_kernel(first, p0, p1, p2, p3, gain, cos_ref, sine_ref, nq, kv, latent_own, whole):
    cols = p0.shape[1]
    for k, piece in enumerate((p0, p1, p2, p3)):
        at = ((first[0] + k) & 3) * cols
        whole[:, pl.ds(pl.multiple_of(at, cols), cols)] = piece[...]
    latent = whole[:, :QLAT].astype(F32)
    nq[...] = (latent * rms_scale(latent) * gain[...]).astype(BF)
    keys = whole[:, QLAT : QLAT + HDIM].astype(F32)
    kv[:, :HDIM] = turn(keys, cos_ref[...], sine_ref[...]).astype(BF)
    kv[:, HDIM:] = whole[:, QLAT + HDIM :]
    rows = latent_own.shape[0]
    latent_own[...] = whole[pl.ds(pl.multiple_of(first[0] * rows, rows), rows), :QLAT]


def project(first, pieces, gain, cos_table, sine_table):
    line, cols = pieces[0].shape
    return pl.pallas_call(
        project_kernel,
        in_specs=[SMEM_SPEC] + [VMEM_SPEC] * 7,
        out_specs=[VMEM_SPEC] * 3,
        out_shape=[shape((line, QLAT), BF), shape((line, 2 * HDIM), BF), shape((line // 4, QLAT), BF)],
        scratch_shapes=[pltpu.VMEM((line, 4 * cols), BF)],
        compiler_params=BIG,
        cost_estimate=cost(3.5),
    )(first, *pieces, gain, cos_table, sine_table)


def hidden_kernel(
    place, p0, p1, p2, p3, back, blocks, n2, o0, o1, o2, o3, hidden, turned, down, grads, weights, sems, out_sems
):
    half_cols, wide = blocks.shape[2] // 2, blocks.shape[3]
    count = weights.shape[1]
    copies = [[], []]
    for half in (0, 1):
        for slot in (0, 1):
            for d in range(blocks.shape[0] // 2):
                src = blocks.at[2 * d + (place[3] ^ slot), :, pl.ds(half * half_cols, half_cols)]
                row = (2 * half + slot) * half_cols
                dst = weights.at[:, pl.ds(row, half_cols), pl.ds(d * wide, wide)]
                at = half * 32 + len(copies[half])
                copies[half].append(pltpu.make_async_copy(src, dst, sems.at[at]))
    for copy in copies[0] + copies[1]:
        copy.start()
    outs = []
    for half in (0, 1):
        rows = pl.ds(half * 2 * half_cols, 2 * half_cols)
        outs.append(pltpu.make_async_copy(weights.at[2, rows], down.at[rows], out_sems.at[half]))
    lay_rows(None, (p0, p1, p2, p3), n2)

    def ready(half):
        for copy in copies[half]:
            copy.wait()
        outs[half].start()

    ready(0)
    for start in range(0, count, 256):
        size = min(256, count - start)
        if start <= 2 * half_cols < start + size:
            ready(1)
        rows = pl.ds(start, size)
        gate = mm_nt(n2[...], weights[0, rows])
        up = mm_nt(n2[...], weights[1, rows])
        grad = mm_nt(back[...], weights[2, rows])
        s = jax.nn.sigmoid(gate)
        silu = gate * s
        parts = [
            (grad * up * s * (1.0 + gate * (1.0 - s))).astype(BF),
            (grad * silu).astype(BF),
            (silu * up).astype(BF),
        ]
        grads[:, rows] = parts[0]
        grads[:, pl.ds(count + start, size)] = parts[1]
        quarter = hidden.shape[0] // 4
        for k in range(4):
            at = ((place[4] + k) & 3) * quarter
            hidden[pl.ds(pl.multiple_of(at, quarter), quarter), rows] = parts[2][k * quarter : (k + 1) * quarter]
        for m, tile in enumerate(parts):
            turned[m, rows] = tile.T
    rows = o0.shape[0]
    for start in range(0, n2.shape[1], 256):
        cols = pl.ds(start, 256)
        got = mm(grads[:, :count], weights[0, :, cols]) + mm(grads[:, count:], weights[1, :, cols])
        for k, part in enumerate((o0, o1, o2, o3)):
            part[:, cols] = got[k * rows : (k + 1) * rows].astype(BF)
    for copy in outs:
        copy.wait()


def hidden_units(place, n2_pieces, back_rows, blocks):
    line = back_rows.shape[0]
    cols, wide = blocks.shape[2:]
    whole = blocks.shape[0] // 2 * wide
    return pl.pallas_call(
        hidden_kernel,
        in_specs=[SMEM_SPEC] + [VMEM_SPEC] * 5 + [ANY_SPEC],
        out_specs=[VMEM_SPEC] * 7 + [ANY_SPEC],
        out_shape=[shape((line, whole), BF)]
        + [shape((line // 4, whole), BF)] * 4
        + [
            shape((line, 2 * cols), BF),
            shape((3, 2 * cols, line), BF),
            shape((2 * cols, whole), BF),
        ],
        scratch_shapes=[
            pltpu.VMEM((line, 4 * cols), BF),
            pltpu.VMEM((3, 2 * cols, whole), BF),
            pltpu.SemaphoreType.DMA((64,)),
            pltpu.SemaphoreType.DMA((2,)),
        ],
        compiler_params=BIG,
        cost_estimate=cost(22),
    )(place, *n2_pieces, back_rows, blocks)


def spot(place, slot, step):
    e = 2 * (step >> 2) + slot
    dx = step & 3
    first = place[2] == 0
    return jnp.where(first, e, dx), jnp.where(first, dx, e)


def hidden_grads_kernel(place, own, other, n2_own, n2_other, back_own, back_other, *refs):
    outs, buf, sems = refs[:4], refs[4], refs[5]
    mat, step = pl.program_id(0), pl.program_id(1)
    at = mat * pl.num_programs(1) + step
    turn_of = lax.rem(at, 2)
    rows, wide = outs[0].shape[3:]
    pair = pair_at(place, step >> 2, step & 3)

    def copy_to(turn, slot, i, j):
        return pltpu.make_async_copy(buf.at[turn, slot], outs[i].at[j, :, mat], sems.at[turn, slot])

    @pl.when(at >= 2)
    def _():
        for slot in (0, 1):
            copy_to(turn_of, slot, 0, 0).wait()

    def put(rows_own, rows_other):
        terms = mm(own[0], lanes(rows_own, pair, 2 * wide)) + mm(other[0], lanes(rows_other, pair, 2 * wide))
        terms = terms.astype(BF)
        for slot in (0, 1):
            for k in (0, 1):
                buf[turn_of, slot, k] = terms[slot * rows : (slot + 1) * rows, k * wide : (k + 1) * wide]

    @pl.when(mat < 2)
    def _():
        put(n2_own, n2_other)

    @pl.when(mat == 2)
    def _():
        put(back_own, back_other)

    for slot in (0, 1):
        i, j = spot(place, slot, step)
        for n in range(4):

            @pl.when(i == n)
            def _():
                copy_to(turn_of, slot, n, j).start()

    @pl.when(at == pl.num_programs(0) * pl.num_programs(1) - 1)
    def _():
        for turn in (0, 1):
            for slot in (0, 1):
                copy_to(turn, slot, 0, 0).wait()


def hidden_grads(place, own, other, n2_own, n2_other, back_own, back_other):
    cols, line = other.shape[1:]
    wide = n2_own.shape[1] // 16
    own_spec = pl.BlockSpec((1, cols, line), lambda m, t, place: (m, place[2], 0))
    other_spec = pl.BlockSpec((1, cols, line), lambda m, t, place: (m, 0, 0))
    rows_spec = pl.BlockSpec(n2_own.shape, lambda m, t, place: (0, 0))
    return pl.pallas_call(
        hidden_grads_kernel,
        grid_spec=pltpu.PrefetchScalarGridSpec(
            num_scalar_prefetch=1,
            grid=(3, 8),
            in_specs=[own_spec, other_spec] + [rows_spec] * 4,
            out_specs=[ANY_SPEC] * 4,
            scratch_shapes=[
                pltpu.VMEM((2, 2, 2, cols // 2, wide), BF),
                pltpu.SemaphoreType.DMA((2, 2)),
            ],
        ),
        out_shape=[shape((4, 2, 3, cols // 2, wide), BF)] * 4,
        compiler_params=BIG,
        cost_estimate=cost(23),
    )(place, own, other, n2_own, n2_other, back_own, back_other)


def att_grads_kernel(place, dh_own, dh_other, nq_own, nq_other, a_own, a_other, g_own, g_other, dst):
    rows = dh_own.shape[1]
    wide = dst.shape[4]
    both = lambda a, b: jnp.concatenate([a[...], b[...]], axis=0)
    out_terms = mm_tn(both(dh_own, dh_other), both(a_own, a_other)).astype(BF)
    query_terms = mm_tn(both(nq_own, nq_other), both(g_own, g_other)).astype(BF)
    for h in range(dst.shape[2]):
        cols = slice(h * wide, (h + 1) * wide)
        dst[0, 0, h, :rows] = out_terms[:, cols]
        dst[0, 0, h, rows:] = query_terms[:, cols]


def att_grads(place, dh, nq, attended, grad_pre):
    line = dh[0].shape[0]
    out_rows, query_rows = dh[0].shape[1] // 8, nq[0].shape[1] // 8
    cols = attended[0].shape[1] // 4
    pair = lambda wide: pl.BlockSpec((line, wide), lambda s, t, place: (0, pair_at(place, t >> 2, t & 3)))
    half = pl.BlockSpec((line, cols), lambda s, t, place: (0, 2 * s + place[2]))
    return pl.pallas_call(
        att_grads_kernel,
        grid_spec=pltpu.PrefetchScalarGridSpec(
            num_scalar_prefetch=1,
            grid=(2, 8),
            in_specs=[pair(out_rows)] * 2 + [pair(query_rows)] * 2 + [half] * 4,
            out_specs=pl.BlockSpec(
                (1, 1, 2, out_rows + query_rows, cols // 2),
                lambda s, t, place: spot(place, s, t) + (0, 0, 0),
            ),
        ),
        out_shape=shape((4, 4, 2, out_rows + query_rows, cols // 2), BF),
        compiler_params=BIG,
        cost_estimate=cost(15),
    )(place, *dh, *nq, *attended, *grad_pre)


def lay_rows(first, pieces, out):
    rows = pieces[0].shape[0]
    for k, piece in enumerate(pieces):
        if first is None:
            out[k * rows : (k + 1) * rows] = piece[...]
        else:
            at = ((first + k) & 3) * rows
            out[pl.ds(pl.multiple_of(at, rows), rows)] = piece[...]


def entry_kernel(place, first, p0, p1, p2, p3, own, other, out, rows):
    lay_rows(first[0], (p0, p1, p2, p3), rows)
    total = 0.0
    wide = own.shape[2]
    for dc, buf in enumerate((own, other)):
        for dx in range(4):
            left = [
                lanes(rows, pair_at(place, dyh, dx) * 2 + (place[2] ^ dc), wide) for dyh in (0, 1)
            ]
            total = total + mm(jnp.concatenate(left, axis=1), buf[dx].reshape(2 * wide, -1))
    out[...] = total.astype(BF)


def entry_project(place, first, pieces, own, other):
    rows, width = pieces[0].shape
    return pl.pallas_call(
        entry_kernel,
        in_specs=[SMEM_SPEC] * 2 + [VMEM_SPEC] * 6,
        out_specs=[VMEM_SPEC] * 2,
        out_shape=[shape((4 * rows, own.shape[3]), BF), shape((4 * rows, width), BF)],
        compiler_params=BIG,
        cost_estimate=cost(5),
    )(place, first, *pieces, own, other)


def entry_grads_kernel(place, n1_own, n1_other, df_own, df_other, dst):
    wide = dst.shape[2]
    right = jnp.concatenate([df_own[...], df_other[...]], axis=0)
    for dyh in (0, 1):
        for dx in range(4):
            block = pair_at(place, dyh, dx) * 2 + place[2]
            left = jnp.concatenate([lanes(n1_own, block, wide), lanes(n1_other, block, wide)], axis=0)
            dst[dyh, dx] = mm_tn(left, right).astype(BF)


def entry_grads(place, n1_own, n1_other, df_own, df_other):
    return pl.pallas_call(
        entry_grads_kernel,
        in_specs=[SMEM_SPEC] + [VMEM_SPEC] * 4,
        out_specs=VMEM_SPEC,
        out_shape=shape((2, 4, n1_own.shape[1] // 16, df_own.shape[1]), BF),
        compiler_params=BIG,
        cost_estimate=cost(4.5),
    )(place, n1_own, n1_other, df_own, df_other)


def entry_step_kernel(first, m0, m1, m2, m3, weight, moment, squares, average, *outs):
    rows = weight.shape[0]
    cols = m0.shape[1]
    for k, message in enumerate((m0, m1, m2, m3)):
        at = ((first[0] + k) & 3) * cols
        place = pl.ds(pl.multiple_of(at, cols), cols)
        new = full_step(
            weight[:, place], moment[:, place], squares[:, place], average[:, place],
            message[:rows].astype(F32), ENTRY_RATE, DECAY,
        )
        for out, value in zip(outs, new):
            out[:, place] = value


def entry_step(first, messages, weight, moment, squares, average):
    return pl.pallas_call(
        entry_step_kernel,
        in_specs=[SMEM_SPEC] + [VMEM_SPEC] * 8,
        out_specs=[VMEM_SPEC] * 5,
        out_shape=[shape(weight.shape, F32)] * 5,
        compiler_params=BIG,
        cost_estimate=cost(4),
    )(first, *messages, weight, moment, squares, average)


def finish_kernel(grad_first, whole, x_ref, mid_ref, gain_ref, grad_out, gain_row):
    grad = mm_nt(grad_first[...], whole[...])
    x = x_ref[...].astype(F32)
    scale = rms_scale(x)
    unit = x * scale
    gain_row[...] = jnp.sum(grad * unit, axis=0, keepdims=True)
    grad_out[...] = mid_ref[...] + norm_back(grad, unit, scale, gain_ref[...])


def finish(grad_first, whole, tokens, grad_middle, gain_one):
    rows = tokens.shape[0]
    return pl.pallas_call(
        finish_kernel,
        in_specs=[VMEM_SPEC] * 5,
        out_specs=[VMEM_SPEC] * 2,
        out_shape=[shape((rows, D), F32), shape((1, D), F32)],
        compiler_params=BIG,
        cost_estimate=cost(6.5),
    )(grad_first, whole, tokens, grad_middle, gain_one)


def turn(values, cos_table, sine_table):
    half = values.shape[1] // 2
    left, right = values[:, :half], values[:, half:]
    return jnp.concatenate(
        [left * cos_table - right * sine_table, left * sine_table + right * cos_table], axis=1
    )


def give_rows(first, source, pieces):
    rows = pieces[0].shape[0]
    for k, piece in enumerate(pieces):
        at = ((first + k) & 3) * rows
        piece[...] = source[pl.ds(pl.multiple_of(at, rows), rows)].astype(piece.dtype)


def attend_kernel(
    info, nq, query_w, kv_own, kv_other, starts, cos_ref, sine_ref, out_w,
    q_out, out, w_own, w_other, o0, o1, o2, o3, branch,
):
    yl = info[0]
    head = pl.program_id(0)
    line = nq.shape[0]
    block = 128
    queries = turn(mm(nq[...], query_w[...]), cos_ref[...], sine_ref[...]).astype(BF)
    q_out[...] = queries
    scale = HDIM ** (-0.5)

    def work(with_other):
        for at in range(0, line, block):
            end = at + block
            q = queries[at:end]
            first = starts[at:end] - yl * line
            own = mm_nt(q, kv_own[:end, :HDIM]) * scale
            spot = lax.broadcasted_iota(jnp.int32, (block, end), 1)
            row = at + lax.broadcasted_iota(jnp.int32, (block, end), 0)
            own = jnp.where((spot <= row) & (spot >= first), own, MASKED)
            top = jnp.max(own, axis=1, keepdims=True)
            if with_other:
                far = mm_nt(q, kv_other[:, :HDIM]) * scale
                far_spot = lax.broadcasted_iota(jnp.int32, (block, line), 1) - line
                far = jnp.where(far_spot >= first, far, MASKED)
                top = jnp.maximum(top, jnp.max(far, axis=1, keepdims=True))
                far = jnp.exp(far - top)
            own = jnp.exp(own - top)
            total = jnp.sum(own, axis=1, keepdims=True)
            if with_other:
                total = total + jnp.sum(far, axis=1, keepdims=True)
            share = 1.0 / total
            own = (own * share).astype(BF)
            w_own[0, at:end, :end] = own
            if end < line:
                w_own[0, at:end, end:] = jnp.zeros((block, line - end), BF)
            result = mm(own, kv_own[:end, HDIM:])
            if with_other:
                far = (far * share).astype(BF)
                w_other[0, at:end] = far
                result = result + mm(far, kv_other[:, HDIM:])
            out[at:end] = result.astype(BF)

    @pl.when(yl == 0)
    def _():
        work(False)

    @pl.when(yl == 1)
    def _():
        work(True)

    part = mm_nt(out[...], out_w[...])

    @pl.when(head == 0)
    def _():
        branch[...] = part

    @pl.when(head > 0)
    def _():
        branch[...] += part

    @pl.when(head == pl.num_programs(0) - 1)
    def _():
        give_rows(info[1], branch, (o0, o1, o2, o3))


def attend(info, nq, query_low, kv_own, kv_other, starts, cos_table, sine_table, out_low):
    line = nq.shape[0]
    width = query_low.shape[1]
    heads = width // HDIM
    whole = lambda v: pl.BlockSpec(v.shape, lambda h: (0, 0))
    head = pl.BlockSpec((line, HDIM), lambda h: (0, h))
    weight = lambda v: pl.BlockSpec((v.shape[0], HDIM), lambda h: (0, h))
    weights = pl.BlockSpec((1, line, line), lambda h: (h, 0, 0))
    piece = (line // 4, out_low.shape[0])
    return pl.pallas_call(
        attend_kernel,
        grid=(heads,),
        in_specs=[SMEM_SPEC, whole(nq), weight(query_low)]
        + [whole(v) for v in (kv_own, kv_other, starts, cos_table, sine_table)]
        + [weight(out_low)],
        out_specs=[head, head, weights, weights] + [pl.BlockSpec(piece, lambda h: (0, 0))] * 4,
        out_shape=[shape((line, width), BF)] * 2
        + [shape((heads, line, line), BF)] * 2
        + [shape(piece, BF)] * 4,
        scratch_shapes=[pltpu.VMEM((line, out_low.shape[0]), F32)],
        compiler_params=BIG,
        cost_estimate=cost(16),
    )(info, nq, query_low, kv_own, kv_other, starts, cos_table, sine_table, out_low)


def attend_back_kernel(
    info, p0, p1, p2, p3, out_w, out, queries, kv_own, kv_other, w_own, w_other, cos_ref, sine_ref, query_w,
    dh, grad_q, o0, o1, o2, o3, scores, k_own, v_own, k_far, v_far, grad_nq, sums,
):
    yl = info[0]
    head = pl.program_id(0)
    line = queries.shape[0]
    block = 128
    scale = HDIM ** (-0.5)

    @pl.when(head == 0)
    def _():
        lay_rows(info[1], (p0, p1, p2, p3), dh)
        for ref in (k_own, v_own, k_far, v_far, grad_nq):
            ref[...] = jnp.zeros_like(ref)

    g = mm(dh[...], out_w[...]).astype(BF)
    delta = jnp.sum(g.astype(F32) * out[...].astype(F32), axis=1, keepdims=True)

    def work(with_other):
        for at in range(0, line, block):
            end = at + block
            own = mm_nt(g[at:end], kv_own[:end, HDIM:]) - delta[at:end]
            own = (w_own[0, at:end, :end].astype(F32) * own).astype(BF)
            scores[at:end, :end] = own
            grad = mm(own, kv_own[:end, :HDIM])
            if with_other:
                far = mm_nt(g[at:end], kv_other[:, HDIM:]) - delta[at:end]
                far = (w_other[0, at:end].astype(F32) * far).astype(BF)
                scores[at:end, line:] = far
                grad = grad + mm(far, kv_other[:, :HDIM])
            grad_q[at:end] = turn(grad * scale, cos_ref[at:end], -sine_ref[at:end]).astype(BF)
        for at in range(0, line, block):
            end = at + block
            k_own[at:end] += mm_tn(scores[at:, at:end], queries[at:])
            v_own[at:end] += mm_tn(w_own[0, at:, at:end], g[at:])
        if with_other:
            k_far[...] += mm_tn(scores[:, line:], queries[...])
            v_far[...] += mm_tn(w_other[0], g)

    @pl.when(yl == 0)
    def _():
        work(False)

    @pl.when(yl == 1)
    def _():
        work(True)

    grad_nq[...] += mm_nt(grad_q[...], query_w[...])

    @pl.when(head == pl.num_programs(0) - 1)
    def _():
        width = grad_nq.shape[1]
        sums[:, :width] = grad_nq[...]
        for i, (ref, factor) in enumerate(((k_own, scale), (v_own, 1.0), (k_far, scale), (v_far, 1.0))):
            sums[:, width + i * HDIM : width + (i + 1) * HDIM] = ref[...] * factor
        give_rows(info[1], sums, (o0, o1, o2, o3))


def attend_back(
    info, dh_pieces, out_low, out, queries, kv_own, kv_other, w_own, w_other, cos_table, sine_table, query_low
):
    line, width = queries.shape
    heads = width // HDIM
    latent = query_low.shape[0]
    whole = lambda v: pl.BlockSpec(v.shape, lambda h: (0, 0))
    head = pl.BlockSpec((line, HDIM), lambda h: (0, h))
    weight = lambda v: pl.BlockSpec((v.shape[0], HDIM), lambda h: (0, h))
    weights = pl.BlockSpec((1, line, line), lambda h: (h, 0, 0))
    piece = (line // 4, latent + 4 * HDIM)
    rows = (line, out_low.shape[0])
    return pl.pallas_call(
        attend_back_kernel,
        grid=(heads,),
        in_specs=[SMEM_SPEC]
        + [whole(v) for v in dh_pieces]
        + [weight(out_low), head, head, whole(kv_own), whole(kv_other), weights, weights]
        + [whole(cos_table), whole(sine_table), weight(query_low)],
        out_specs=[pl.BlockSpec(rows, lambda h: (0, 0)), head] + [pl.BlockSpec(piece, lambda h: (0, 0))] * 4,
        out_shape=[shape(rows, BF), shape((line, width), BF)] + [shape(piece, BF)] * 4,
        scratch_shapes=[pltpu.VMEM((line, 2 * line), BF)]
        + [pltpu.VMEM((line, HDIM), F32)] * 4
        + [pltpu.VMEM((line, latent), F32), pltpu.VMEM((line, piece[1]), F32)],
        compiler_params=BIG,
        cost_estimate=cost(16),
    )(
        info, *dh_pieces, out_low, out, queries, kv_own, kv_other, w_own, w_other, cos_table, sine_table, query_low
    )


def local(
    tokens,
    cotangent,
    doc_lengths,
    entry_weight,
    entry_first,
    entry_second,
    entry_average,
    query_weight,
    query_first,
    query_second,
    query_average,
    out_weight,
    out_first,
    out_second,
    out_average,
    ffn_weight,
    ffn_first,
    ffn_second,
    ffn_average,
    norm_gains,
    gains_first,
    gains_second,
    gains_average,
):
    rows = tokens.shape[0]
    line = 4 * rows
    z, yl, c = lax.axis_index("z"), lax.axis_index("yl"), lax.axis_index("c")
    place = jnp.stack([lax.axis_index(a) for a in ("yh", "x", "c", "yl", "z")]).astype(jnp.int32)
    wide = D // 16
    ffn_cols = ffn_weight.shape[2]
    half_cols = ffn_cols // 2
    entry_cols = entry_weight.shape[1]
    slot_cols = entry_cols // 4
    head_cols = query_weight.shape[1]
    gain_one = 1.0 + norm_gains[None, :D]
    gain_query = 1.0 + norm_gains[D : D + QLAT]
    gain_two = 1.0 + norm_gains[None, D + QLAT :]

    ffn_low = jnp.transpose(ffn_weight, (1, 2, 0)).astype(BF)

    inputs = tokens.astype(F32)
    scale_one = rms_scale(inputs)
    normed_one = (inputs * scale_one * gain_one).astype(BF)
    first = z[None].astype(jnp.int32)
    start = jnp.zeros((1,), jnp.int32)
    n1_near = ring_near(normed_one)

    entry_low = entry_weight.astype(BF)
    slot = lax.dynamic_slice_in_dim(entry_low, z * slot_cols, slot_cols, 1)
    slot = jnp.stack([slot, from_y(slot, 3)])
    slot = jnp.stack([slot] + [from_x(slot, k) for k in (1, 2, 3)])
    n1_pieces = ring_pieces(normed_one, n1_near)
    slot, *n1_pieces = tie(slot, *n1_pieces)
    slot_other = from_c(slot)

    att_half = head_cols // 2
    halves = [
        (out_weight[:, h * att_half : (h + 1) * att_half], query_weight[:, h * att_half : (h + 1) * att_half])
        for h in (0, 1)
    ]
    keep, give = by_core(*[jnp.concatenate(h, axis=0).astype(BF) for h in halves])
    got = from_c(give)
    att_0, att_1 = by_core(keep, got)
    att_own = jnp.concatenate([att_0[:wide], att_1[:wide], att_0[wide:], att_1[wide:]], axis=0)
    att_near = gather_near(att_own)

    f_slot, n1_rows = entry_project(place, first, n1_pieces, slot, slot_other)
    f_slot, doc_lengths, att_near = tie(f_slot, doc_lengths, att_near)
    *tied, ffn_low = tie(*gather_far(att_near), *ring_pieces(f_slot), ffn_low)
    att_far, f_pieces = tied[:4], tied[4:]
    ffn_all = lax.all_gather(ffn_low, PLANE, axis=0, tiled=False)
    places_all, segment_all, offset_all = doc_layout(doc_lengths[0], 2 * line)
    line_offset = lax.dynamic_slice_in_dim(offset_all, yl * line, line)
    line_places = yl * line + jnp.arange(line, dtype=jnp.int32)
    starts = (line_places - line_offset)[:, None]
    cos_line, sine_line = rope_tables(line_offset, HDIM // 2)
    query_rows, kv_own, latent_own = project(
        first, f_pieces, gain_query[None], cos_line, sine_line
    )
    kv_other = from_y(kv_own, 1)
    info = place[3:]
    out_low, query_low = att_weights(place, att_far + [from_c(v) for v in att_far])
    out_low, cot_late = tie(out_low, cotangent)
    back_pieces = line_pieces(cot_late)
    queries, attended, w_own, w_other, *branch = attend(
        info, query_rows, query_low, kv_own, kv_other, starts, cos_line, sine_line, out_low
    )

    *tied, back_pieces[0] = tie(*branch, *back_pieces[1:], back_pieces[0])
    branch, back_pieces[1:] = tied[:4], tied[4:]
    *branch, back_rows = tie(*line_sum(*branch), place_rows(back_pieces, start))
    middle = inputs + total(branch)
    scale_two = rms_scale(middle)
    unit_two = middle * scale_two
    normed_two = (unit_two * gain_two).astype(BF)

    n2_pieces = ring_pieces(normed_two)
    back_other, query_other, attended_other = from_c(back_rows), from_c(query_rows), from_c(attended)
    back_other, query_other, attended_other, entry_low, ffn_all, *n2_pieces = tie(
        back_other, query_other, attended_other, entry_low, ffn_all, *n2_pieces
    )
    entry_all = lax.all_gather(entry_low, DP, axis=0, tiled=True)
    n2_rows, *n2_parts, hidden_low, turned, down_low = hidden_units(place, n2_pieces, back_rows, ffn_all)
    turned_away = lax.dynamic_slice_in_dim(turned, (1 - c) * 2 * half_cols, 2 * half_cols, 1)
    ffn_terms = hidden_grads(
        place, turned, from_c(turned_away), n2_rows, from_c(n2_rows), back_rows, back_other
    )
    tied = tie(*line_sum(*n2_parts), *ffn_terms)
    grad_normed_two, ffn_terms = total(tied[:4]), tied[4:]
    ffn_far = far_moves(ffn_terms)
    grad_middle = cotangent.astype(F32) + norm_back(grad_normed_two, unit_two, scale_two, gain_two)
    dh_pieces = line_pieces(grad_middle.astype(BF))
    mixed_part = mm(hidden_low, down_low).astype(BF)
    *dh_pieces, mixed_part, entry_all = tie(*dh_pieces, mixed_part, entry_all)
    mixed = lax.psum_scatter(mixed_part, "z", scatter_dimension=0, tiled=True)
    mixed_out = (middle + mixed.astype(F32)).astype(BF)

    dh_rows, grad_query_pre, *sums = attend_back(
        info, dh_pieces, out_low, attended, queries, kv_own, kv_other, w_own, w_other,
        cos_line, sine_line, query_low,
    )
    *sums, ffn_far[1], ffn_far[2] = tie(*sums, ffn_far[1], ffn_far[2])
    summed = line_sum(*sums)
    pair = lambda v: (v, from_c(v))
    att_terms = att_grads(
        place, pair(dh_rows), (query_rows, query_other), (attended, attended_other), pair(grad_query_pre)
    )
    *summed, att_terms = tie(*summed, att_terms)
    summed = total(summed)
    grad_normed_query = summed[:, :QLAT]
    kv_got = from_y(summed[:, QLAT + 2 * HDIM :].astype(BF), 1)
    kv_got, ffn_far[3] = tie(kv_got, ffn_far[3])
    kv_grad = summed[:, QLAT : QLAT + 2 * HDIM] + kv_got.astype(F32)
    own = lambda v: rows_of(v, 0, rows)
    latent = latent_own.astype(F32)
    scale_query = rms_scale(latent)
    unit_query = latent * scale_query
    grad_latent = norm_back(grad_normed_query, unit_query, scale_query, gain_query)
    grad_first = jnp.concatenate(
        [grad_latent, rotate(kv_grad[:, :HDIM], own(cos_line), -own(sine_line)), kv_grad[:, HDIM:]], axis=1
    ).astype(BF)

    grad_first, *att_terms = tie(grad_first, att_terms)
    att_far = far_moves(att_terms[0])
    input_grad, one_row = finish(grad_first, entry_all, tokens, grad_middle, gain_one)

    gain_terms = jnp.concatenate(
        [
            one_row[0],
            jnp.sum(grad_normed_query * unit_query, axis=0),
            jnp.sum(grad_normed_two * unit_two, axis=0),
        ]
    )
    gain_count = gain_terms.shape[0]
    gain_height = -(-gain_count // (16 * slot_cols)) * 16
    gain_terms = jnp.pad(gain_terms, (0, gain_height * slot_cols - gain_count)).reshape(gain_height, slot_cols)

    def exchange(values, moves, gains):
        sent = [step(jnp.concatenate([v, gains.astype(BF)], axis=0)) for v, step in zip(values, moves)]
        gains = gains + sum(m[-gain_height:].astype(F32) for m in sent)
        return [m[:-gain_height] for m in sent], gains

    cols_of = lambda k: lax.dynamic_slice_in_dim(grad_first, ((z + k) % 4) * slot_cols, slot_cols, 1)
    df_slot = place_rows([cols_of(0)] + [from_z(cols_of(4 - k), k) for k in (1, 2, 3)], first)
    df_slot, att_far[1], att_far[2] = tie(df_slot, att_far[1], att_far[2])
    (df_other,), gains_grad = exchange([df_slot], [from_c], gain_terms)
    entry_terms = entry_grads(place, n1_rows, from_c(n1_rows), df_slot, df_other)
    got, gains_grad = exchange(
        [entry_terms[:, k].reshape(2 * wide, slot_cols) for k in (1, 2, 3)],
        [lambda v, k=k: from_x(v, 4 - k) for k in (1, 2, 3)],
        gains_grad,
    )
    *got, att_far[3] = tie(*got, att_far[3])
    low = jnp.concatenate([total(v).astype(BF).reshape(4, -1, wide) for v in (ffn_far, att_far)], axis=1)
    near = sum_near(low)
    ffn_rows = 6 * half_cols
    ffn_got = near[:ffn_rows].reshape(2, -1, wide)
    att_got = near[ffn_rows:].reshape(2, 3 * wide, wide)
    for_core = [
        jnp.concatenate(
            [ffn_got[n]]
            + [
                att_got[h, a * wide + n * b : a * wide + (n + 1) * b]
                for h in (0, 1)
                for a, b in ((0, wide), (2, wide // 2))
            ],
            axis=0,
        )
        for n in (0, 1)
    ]
    mine, theirs = by_core(*for_core)
    halves = by_core(mine, from_c(theirs.astype(BF)).astype(F32))
    ffn_rows = ffn_rows // 2
    ffn_grad = jnp.concatenate([v[:ffn_rows].reshape(3, half_cols, wide) for v in halves], axis=1)
    ffn_grad = jnp.transpose(ffn_grad, (2, 0, 1))
    att_grad = jnp.concatenate(
        [v[ffn_rows + h * 3 * wide // 2 :][: 3 * wide // 2] for v in halves for h in (0, 1)], axis=1
    )
    out_grad, query_grad = att_grad[:wide], att_grad[wide:]

    part = sum((v.astype(F32) for v in got), entry_terms[:, 0].reshape(2 * wide, slot_cols).astype(F32))
    low = part.astype(BF).reshape(2, wide, slot_cols)
    got, gains_grad = exchange(
        [low[e >> 1] for e in (1, 2, 3)], [lambda v, e=e: from_y(v, e) for e in (1, 2, 3)], gains_grad
    )
    low = sum((v.astype(F32) for v in got), part[:wide]).astype(BF)
    own_message = jnp.concatenate([low, gains_grad.astype(BF)], axis=0)
    messages = [own_message] + [from_z(own_message, k) for k in (1, 2, 3)]
    gains_grad = gains_grad + sum(m[-gain_height:].astype(F32) for m in messages[1:])
    gains_grad = gains_grad.reshape(-1)[:gain_count]
    entry_new = entry_step(first, messages, entry_weight, entry_first, entry_second, entry_average)

    return (
        (mixed_out, input_grad)
        + tuple(entry_new)
        + full_step(query_weight, query_first, query_second, query_average, query_grad, QUERY_RATE, DECAY)
        + full_step(out_weight, out_first, out_second, out_average, out_grad, OUT_RATE, DECAY)
        + full_step(ffn_weight, ffn_first, ffn_second, ffn_average, ffn_grad, FFN_RATE, DECAY)
        + full_step(norm_gains, gains_first, gains_second, gains_average, gains_grad, GAIN_RATE, 0.0)
    )


def solution(mesh):
    fine = Mesh(mesh.devices.reshape(tuple(SIZES[a] for a in AXES)), AXES)
    tokens = P(AXES, None)
    entry = P(DP, None)
    middle = P(DP, SEQ)
    ffn = P(DP, None, SEQ)
    gains = P()
    return jax.shard_map(
        local,
        mesh=fine,
        in_specs=(tokens, tokens, entry) + (entry,) * 4 + (middle,) * 8 + (ffn,) * 4 + (gains,) * 4,
        out_specs=(tokens, tokens) + (entry,) * 5 + (middle,) * 10 + (ffn,) * 5 + (gains,) * 5,
        check_vma=False,
    )
```
